128 devices in a mesh: tok: 4 (over z), lat: 32 (over y, x, core).
Axes of the slice: x: 4, y: 4, z: 4, core: 2. Of those that a mesh axis runs over, the one named last changes fastest.
Arguments:
- tokens: bfloat16 [1024, 4096], P('tok'), may hold values from -6 to 6
- indices: int32 [1024, 64], replicated, may hold values from 0 to 65535, as said below
- enc_weight: bfloat16 [4096, 65536], P('tok', 'lat'), may hold values from -0.375 to 0.375
- dec_weight: bfloat16 [65536, 4096], P('lat', 'tok'), may hold values from -0.09375 to 0.09375
- enc_bias: float32 [65536], P('lat'), may hold values from -6 to 6
- dec_bias: float32 [4096], P('tok'), may hold values from -3 to 3
Outputs:
- enc_grad: bfloat16 [4096, 65536], P('tok', 'lat')
- dec_grad: bfloat16 [65536, 4096], P('lat', 'tok')
- enc_bias_grad: float32 [65536], P('lat')
- dec_bias_grad: float32 [4096], P('tok')
The draws below stay inside these ranges and needn't reach their ends.
Inputs may be any that keep to these rules, and one draw needn't show every extreme that they name: `indices`: in every row the 64 entries are distinct, and entry s leaves the remainder s when divided by 64.
All inputs are finite; a program needn't handle non-finite values.
Results may differ from the reference program's by a relative error of at most 0.0058.
Values may be sent and summed in bfloat16 or wider, within the bound.
A program may use at most 64 MiB of HBM per device.

```python
import math
import jax
import jax.numpy as jnp
from jax import lax

D = 4096
LAT = 65536
K = 64
TOKENS = 1024


def draw_indices(key, part):
    key = jax.random.fold_in(key, 7)
    key_one, key_two, key_three = jax.random.split(key, 3)
    band_size = LAT // K
    draw_one = jax.random.randint(key_one, (TOKENS, K), 0, band_size)
    draw_two = jax.random.randint(key_two, (TOKENS, K), 0, band_size)
    offsets = jnp.minimum(draw_one, draw_two)
    ranking = jax.random.permutation(key_three, TOKENS)
    offsets = offsets.at[:, K - 1].set(jnp.where(ranking == 0, band_size - 1, offsets[:, K - 1]))
    offsets = offsets.at[:, 0].set(jnp.where(ranking == 1, 0, offsets[:, 0]))
    slot_ids = jnp.arange(K, dtype=jnp.int32)
    return (slot_ids[None, :] + K * offsets).astype(jnp.int32)


def steps_of(own_key, shape, cuts, low, largest):
    factor_of = 1.0
    for position, blocks in cuts:
        draws = jax.random.uniform(jax.random.fold_in(jax.random.fold_in(own_key, 6), position), (blocks,), jnp.float32, low / len(cuts), largest / len(cuts))
        factor_of = factor_of * jnp.repeat(jnp.exp(draws), shape[position] // blocks).reshape((-1,) + (1,) * (len(shape) - 1 - position))
    return factor_of


def bell_draw(key, shape, scale, reach, pieces=(), kind=jnp.bfloat16):
    result = jax.random.normal(key, shape, jnp.float32) * scale
    if len(pieces) > 0:
        result = steps_of(key, shape, pieces, -0.22, 0.18) * result
    return jnp.clip(result, min=-reach, max=reach).astype(kind)


def setup_inputs(seed: int = 0) -> dict:
    splits = jax.random.split(jax.random.key(seed), 7)
    return {
        "tokens": bell_draw(splits[0], (TOKENS, D), 1.0, 6.0, ((0, 4),)),
        "indices": draw_indices(jax.random.fold_in(splits[6], 71), 0),
        "enc_weight": bell_draw(splits[2], (D, LAT), (D // 16) ** -0.5, 0.375, ((0, 4), (1, 32))),
        "dec_weight": bell_draw(splits[3], (LAT, D), D ** -0.5, 0.09375, ((0, 32), (1, 4))),
        "enc_bias": bell_draw(splits[4], (LAT,), 1.0, 6.0, ((0, 32),), jnp.float32),
        "dec_bias": bell_draw(splits[5], (D,), 0.5, 3.0, ((0, 4),), jnp.float32),
    }


def reference(tokens, indices, enc_weight, dec_weight, enc_bias, dec_bias):
    tok_total, width_dim = tokens.shape
    blk_rows = math.gcd(tok_total, 64)
    blocks = tok_total // blk_rows
    tok_blocks = tokens.reshape(blocks, blk_rows, width_dim)
    idx_blocks = indices.reshape(blocks, blk_rows, K)

    def forward(inputs):
        rows_x, rows_idx = inputs
        enc_cols = jnp.take(enc_weight, rows_idx, axis=1).astype(jnp.float32)
        pre_acts = jnp.einsum("td,dtk->tk", rows_x.astype(jnp.float32), enc_cols) + enc_bias[rows_idx]
        code_vals = lax.optimization_barrier(pre_acts.astype(jnp.bfloat16))
        dec_rows = dec_weight[rows_idx].astype(jnp.float32)
        recon_sum = dec_bias[None, :] + jnp.einsum("tk,tkd->td", code_vals.astype(jnp.float32), dec_rows)
        error_full = recon_sum - rows_x.astype(jnp.float32)
        error_half = lax.optimization_barrier(error_full.astype(jnp.bfloat16))
        code_grad = jnp.einsum("td,tkd->tk", error_half.astype(jnp.float32), dec_rows)
        return code_vals, error_full, error_half, code_grad

    code_vals, error_full, error_half, code_grad = lax.map(forward, (tok_blocks, idx_blocks))
    dec_bias_grad = jnp.sum(error_full.reshape(-1, width_dim), axis=0)
    enc_bias_grad = jnp.zeros((LAT,), jnp.float32).at[indices.reshape(-1)].add(code_grad.reshape(-1))
    code_half = lax.optimization_barrier(code_grad.astype(jnp.bfloat16))

    def add_dec(grad_acc, inputs):
        rows_idx, rows_code, rows_err = inputs
        terms = rows_code.astype(jnp.float32)[:, :, None] * rows_err.astype(jnp.float32)[:, None, :]
        return grad_acc.at[rows_idx.reshape(-1)].add(terms.reshape(-1, width_dim)), 0

    def add_enc(grad_acc, inputs):
        rows_idx, rows_code, rows_x = inputs
        terms = rows_code.astype(jnp.float32)[:, :, None] * rows_x.astype(jnp.float32)[:, None, :]
        return grad_acc.at[rows_idx.reshape(-1)].add(terms.reshape(-1, width_dim)), 0

    dec_acc, unused_one = lax.scan(add_dec, jnp.zeros((LAT, width_dim), jnp.float32), (idx_blocks, code_vals, error_half))
    enc_acc, unused_two = lax.scan(add_enc, jnp.zeros((LAT, width_dim), jnp.float32), (idx_blocks, code_half, tok_blocks))
    return enc_acc.T.astype(jnp.bfloat16), dec_acc.astype(jnp.bfloat16), enc_bias_grad, dec_bias_grad
```

```python
import functools

import jax
import jax.numpy as jnp
from jax import lax
from jax.experimental import pallas as pl
from jax.experimental.pallas import tpu as pltpu
from jax.sharding import PartitionSpec as P

MESH = pl.DeviceIdType.MESH
F32, BF16, I32 = jnp.float32, jnp.bfloat16, jnp.int32
NT = (((1,), (1,)), ((), ()))
PLANE = tuple((dy, dx) for dy in range(4) for dx in range(4))
ORDER = (1, 3, 2)


def exchange(
    tokens, idx_t, enc, dec, enc_bias, dec_bias,
    cols_out, dec_grad_out, grad_out, bias_out,
    cols, enc_v, dec_v, key, key_t, picked, own_pre, pre_send, pre_recv,
    codes, code2, codes_t, dense, sib_send, sib_recv, part, rs_send, rs_recv,
    err, grad_part, grad_recv, dec_grad_v,
    sem_local, sem_a, sem_f, sem_b, sem_c, sem_s, sem_r, sem_g, sem_h, sem_d, sem_e, sem_o,
):
    z, lat = lax.axis_index("tok"), lax.axis_index("lat")
    y, x, core = lat // 8, (lat // 2) % 4, lat % 2
    other = 1 - core
    sibling = (z, lat + 1 - 2 * core)

    def along(offset):
        return lax.rem(z + offset, 4)

    def in_plane(dy, dx):
        return (z, lax.rem(y + dy, 4) * 8 + lax.rem(x + dx, 4) * 2 + core)

    def remote(src, dst, sems, index, device):
        return pltpu.make_async_remote_copy(
            src_ref=src, dst_ref=dst, send_sem=sems.at[0, index], recv_sem=sems.at[1, index],
            device_id=device, device_id_type=MESH,
        )

    barrier = pltpu.get_barrier_semaphore()
    peers = [(along(o), lat) for o in ORDER] + [sibling]
    peers += [in_plane(dy, dx) for dy, dx in PLANE if dy or dx]
    for peer in peers:
        pl.semaphore_signal(barrier, inc=1, device_id=peer, device_id_type=MESH)

    own_cols = pltpu.make_async_copy(
        tokens.at[:, pl.ds(pl.multiple_of(1024 * z, 1024), 1024)],
        cols.at[pl.ds(pl.multiple_of(256 * z, 256), 256)], sem_local.at[0])
    load_enc = pltpu.make_async_copy(enc, enc_v, sem_local.at[1])
    load_dec = pltpu.make_async_copy(dec, dec_v, sem_local.at[2])
    own_cols.start()
    load_enc.start()
    load_dec.start()

    pl.semaphore_wait(barrier, len(peers))

    half_rows = pl.ds(pl.multiple_of(128 * core, 128), 128)

    def block_half(block, which):
        return cols.at[pl.ds(pl.multiple_of(256 * block + 128 * which, 128), 128)]

    sends = {}
    for o in ORDER:
        to = along(o)
        sends[o] = remote(
            tokens.at[half_rows, pl.ds(pl.multiple_of(1024 * to, 1024), 1024)],
            block_half(z, core), sem_a, o, (to, lat))
        sends[o].start()

    band_t = lax.shift_right_logical(idx_t[...], 6) - 32 * lat
    key_t[...] = band_t
    odd = (lax.broadcasted_iota(I32, (128, 128), 1) >= 64).astype(I32)
    low = lax.broadcasted_iota(I32, (128, 128), 1) < 64
    for g in range(8):
        piece = band_t[:, 128 * g:128 * g + 128]
        key[128 * g:128 * g + 128, :] = jnp.concatenate([piece, piece], axis=0).T - odd

    own_cols.wait()
    load_enc.wait()

    def pre_block(block, with_bias):
        rows = pl.ds(pl.multiple_of(256 * block, 256), 256)
        picked[...] = jnp.zeros_like(picked)

        @pl.loop(0, 4)
        def _(n):
            base = pl.multiple_of(512 * n, 512)
            scores = jnp.dot(cols[rows, :], enc_v[:, pl.ds(base, 512)], preferred_element_type=F32)
            if with_bias:
                scores = scores + enc_bias[:, pl.ds(base, 512)]
            where = key[rows, :]
            total = picked[...]
            for j in range(4):
                total += jnp.where(where == 8 * n + 2 * j, scores[:, 128 * j:128 * j + 128], 0.0)
            picked[...] = total

        folded = picked[...]
        folded = folded + pltpu.roll(folded, 64, 1)
        return jnp.where(low, folded[:128], folded[128:])

    own_pre[...] = pre_block(z, True)
    forwards = {}
    returns = {}

    def forward(o):
        block = along(4 - o)
        sends[o].wait_recv()
        forwards[o] = remote(block_half(block, core), block_half(block, core), sem_f, o, sibling)
        forwards[o].start()

    def partial(o):
        block = along(4 - o)
        forwards[o].wait_recv()
        pre_send[o] = pre_block(block, False)
        returns[o] = remote(pre_send.at[o], pre_recv.at[o], sem_b, o, (block, lat))
        returns[o].start()

    forward(1)
    forward(3)
    partial(1)
    partial(3)
    forward(2)
    partial(2)

    store_cols = pltpu.make_async_copy(cols, cols_out, sem_local.at[3])
    store_cols.start()

    total = own_pre[...]
    for o in ORDER:
        returns[o].wait_recv()
        total = total + pre_recv[o]
    codes[z] = total.astype(BF16)
    spread_codes = {}
    for o in ORDER:
        spread_codes[o] = remote(codes.at[z], codes.at[z], sem_c, o, (along(o), lat))
        spread_codes[o].start()
    for o in ORDER:
        spread_codes[o].wait_recv()

    for block in range(4):
        packed = codes[block].astype(F32)
        turned = pltpu.roll(packed, 64, 1)
        for high in range(2):
            both = jnp.where(low, turned, packed) if high else jnp.where(low, packed, turned)
            g = 2 * block + high
            code2[128 * g:128 * g + 128, :] = both
            codes_t[:, 128 * g:128 * g + 128] = both.T[:64]

    load_dec.wait()

    def recon(half, chunk, out):
        for pos in range(2):
            dy = (1 + 2 * chunk + pos) % 4
            rows = pl.ds(pl.multiple_of(512 * half + 128 * lax.rem(y + dy, 4), 128), 128)
            where, values = key[rows, :], code2[rows, :]
            for j in range(16):
                dense[128 * pos:128 * pos + 128, 128 * j:128 * j + 128] = jnp.where(
                    where == 2 * j, values, 0.0).astype(BF16)

        @pl.loop(0, 2)
        def _(n):
            base = pl.ds(pl.multiple_of(512 * n, 512), 512)
            out[chunk, :, base] = jnp.dot(dense[...], dec_v[:, base], preferred_element_type=F32)

    to_sibling = {}

    def give(chunk):
        recon(other, chunk, sib_send)
        to_sibling[chunk] = remote(sib_send.at[chunk], sib_recv.at[chunk], sem_s, chunk, sibling)
        to_sibling[chunk].start()

    scatter = {}

    def finish(chunk):
        to_sibling[chunk].wait_recv()

        @pl.loop(0, 8)
        def _(i):
            rows = pl.ds(pl.multiple_of(32 * i, 32), 32)
            total = part[chunk, rows, :] + sib_recv[chunk, rows, :]
            part[chunk, rows, :] = total
            rs_send[chunk, rows, :] = total.astype(BF16)

        for pos in range(2):
            dy = (1 + 2 * chunk + pos) % 4
            for dx in range(4):
                if dy == 0 and dx == 0:
                    continue
                slot = 4 * dy + dx
                rows = pl.ds(pl.multiple_of(128 * pos + 32 * lax.rem(x + dx, 4), 32), 32)
                scatter[slot] = remote(rs_send.at[chunk, rows], rs_recv.at[slot], sem_r, slot, in_plane(dy, dx))
                scatter[slot].start()

    give(0)
    recon(core, 0, part)
    give(1)
    finish(0)
    recon(core, 1, part)
    finish(1)

    mine = pl.ds(pl.multiple_of(512 * core + 128 * y + 32 * x, 32), 32)
    full = part[1, pl.ds(pl.multiple_of(128 + 32 * x, 32), 32), :]
    full = full + dec_bias[...] - cols[mine, :].astype(F32)
    for slot in range(1, 16):
        scatter[slot].wait_recv()
        full = full + rs_recv[slot].astype(F32)
    err[mine, :] = full.astype(BF16)

    gather = {}
    for dy, dx in PLANE:
        if dy or dx:
            slot = 4 * dy + dx
            gather[slot] = remote(err.at[mine], err.at[mine], sem_g, slot, in_plane(dy, dx))
            gather[slot].start()
    across = {}
    for dy in range(4):
        for dx in range(4):
            if dy or dx:
                gather[4 * dy + dx].wait_recv()
        rows = pl.ds(pl.multiple_of(512 * core + 128 * lax.rem(y + 4 - dy, 4), 128), 128)
        across[dy] = remote(err.at[rows], err.at[rows], sem_h, dy, sibling)
        across[dy].start()

    def code_grad(block):
        rows = pl.ds(pl.multiple_of(256 * block, 256), 256)
        grad_part[block] = jnp.zeros((64, 256), F32)

        @pl.loop(0, 4)
        def _(n):
            lats = pl.ds(pl.multiple_of(512 * n, 512), 512)
            scores = lax.dot_general(dec_v[lats, :], err[rows, :], NT, preferred_element_type=F32)
            where = key_t[:, rows]
            total = grad_part[block]
            for b in range(8):
                total += jnp.where(where == 8 * n + b, scores[64 * b:64 * b + 64, :], 0.0)
            grad_part[block] = total

    code_grad(2 * core)
    code_grad(2 * core + 1)
    for dy in range(4):
        across[dy].wait_recv()
    code_grad(2 * other)
    code_grad(2 * other + 1)

    grads = {}
    for o in ORDER:
        to = along(o)
        grads[o] = remote(grad_part.at[to], grad_recv.at[o], sem_d, o, (to, lat))
        grads[o].start()

    bias_out[...] = jnp.dot(jnp.ones((16, 1024), BF16), err[...], preferred_element_type=F32)[:8]

    def dec_rows(n):
        return pl.ds(pl.multiple_of(256 * n, 256), 256)

    def dec_grads(first, last):
        @pl.loop(first, last)
        def _(n):
            where, values = key_t[...], codes_t[...]
            wide = jnp.concatenate(
                [jnp.where(where == 4 * n + b, values, 0.0).astype(BF16) for b in range(4)], axis=0)
            dec_grad_v[dec_rows(n), :] = jnp.dot(wide, err[...], preferred_element_type=F32).astype(BF16)
            pltpu.make_async_copy(dec_grad_v.at[dec_rows(n)], dec_grad_out.at[dec_rows(n)], sem_o.at[n]).start()

    dec_grads(0, 4)
    total = grad_part[z]
    for o in ORDER:
        grads[o].wait_recv()
        total = total + grad_recv[o]
    grad_out[z] = total
    shares = {}
    for o in ORDER:
        shares[o] = remote(grad_out.at[z], grad_out.at[z], sem_e, o, (along(o), lat))
        shares[o].start()
    dec_grads(4, 8)

    for o in ORDER:
        shares[o].wait()
        for group in (sends, forwards, returns, spread_codes, grads):
            group[o].wait_send()
    for group in (to_sibling, scatter, gather, across):
        for copy in group.values():
            copy.wait_send()
    store_cols.wait()

    @pl.loop(0, 8)
    def _(n):
        pltpu.make_async_copy(dec_grad_v.at[dec_rows(n)], dec_grad_out.at[dec_rows(n)], sem_o.at[n]).wait()


def enc_grads(cols, grad, idx_t, lat_ref, dec_in, enc_out, enc_bias_out, dec_out, grad2, key, sem):
    n = pl.program_id(0)

    @pl.when(n == 0)
    def _():
        pltpu.make_async_copy(dec_in, dec_out, sem).start()
        odd = (lax.broadcasted_iota(I32, (128, 128), 1) >= 64).astype(I32)
        for g in range(8):
            piece = lax.shift_right_logical(idx_t[:, 128 * g:128 * g + 128], 6) - 32 * lat_ref[0]
            key[128 * g:128 * g + 128, :] = jnp.concatenate([piece, piece], axis=0).T - odd
            piece = grad[g // 2, :, 128 * (g % 2):128 * (g % 2) + 128]
            grad2[128 * g:128 * g + 128, :] = jnp.concatenate([piece, piece], axis=0).T

    where, values = key[...], grad2[...]
    wide = [jnp.where(where == 8 * n + 2 * j, values, 0.0) for j in range(4)]
    for j in range(4):
        enc_bias_out[:, 128 * j:128 * j + 128] = jnp.sum(wide[j], axis=0, keepdims=True)
    wide = jnp.concatenate([w.astype(BF16) for w in wide], axis=1)
    enc_out[...] = lax.dot_general(
        cols[...], wide, (((0,), (0,)), ((), ())), preferred_element_type=F32).astype(BF16)

    @pl.when(n == 3)
    def _():
        pltpu.make_async_copy(dec_in, dec_out, sem).wait()


def local(tokens, indices, enc_weight, dec_weight, enc_bias, dec_bias):
    idx_t = indices.T
    vmem = pl.BlockSpec(memory_space=pltpu.VMEM)
    hbm = pl.BlockSpec(memory_space=pl.ANY)
    dma = pltpu.SemaphoreType.DMA
    cols, dec_grad, grad, bias_grad = pl.pallas_call(
        exchange,
        out_shape=[
            jax.ShapeDtypeStruct((1024, 1024), BF16),
            jax.ShapeDtypeStruct((2048, 1024), BF16),
            jax.ShapeDtypeStruct((4, 64, 256), F32),
            jax.ShapeDtypeStruct((8, 1024), F32),
        ],
        in_specs=[hbm, vmem, hbm, hbm, vmem, vmem],
        out_specs=[hbm, hbm, vmem, vmem],
        scratch_shapes=[
            pltpu.VMEM((1024, 1024), BF16),
            pltpu.VMEM((1024, 2048), BF16),
            pltpu.VMEM((2048, 1024), BF16),
            pltpu.VMEM((1024, 128), I32),
            pltpu.VMEM((64, 1024), I32),
            pltpu.VMEM((256, 128), F32),
            pltpu.VMEM((128, 128), F32),
            pltpu.VMEM((4, 128, 128), F32),
            pltpu.VMEM((4, 128, 128), F32),
            pltpu.VMEM((4, 128, 128), BF16),
            pltpu.VMEM((1024, 128), F32),
            pltpu.VMEM((64, 1024), F32),
            pltpu.VMEM((256, 2048), BF16),
            pltpu.VMEM((2, 256, 1024), F32),
            pltpu.VMEM((2, 256, 1024), F32),
            pltpu.VMEM((2, 256, 1024), F32),
            pltpu.VMEM((2, 256, 1024), BF16),
            pltpu.VMEM((16, 32, 1024), BF16),
            pltpu.VMEM((1024, 1024), BF16),
            pltpu.VMEM((4, 64, 256), F32),
            pltpu.VMEM((4, 64, 256), F32),
            pltpu.VMEM((2048, 1024), BF16),
            dma((4,)), dma((2, 4)), dma((2, 4)), dma((2, 4)), dma((2, 4)), dma((2, 2)),
            dma((2, 16)), dma((2, 16)), dma((2, 4)), dma((2, 4)), dma((2, 4)), dma((8,)),
        ],
        compiler_params=pltpu.CompilerParams(
            collective_id=0, has_side_effects=True, vmem_limit_bytes=48 * 2**20),
        name="exchange",
    )(tokens, idx_t, enc_weight, dec_weight, enc_bias[None, :], dec_bias[None, :])

    enc_grad, enc_bias_grad, dec_grad = pl.pallas_call(
        enc_grads,
        grid=(4,),
        out_shape=[
            jax.ShapeDtypeStruct((1024, 2048), BF16),
            jax.ShapeDtypeStruct((1, 2048), F32),
            jax.ShapeDtypeStruct((2048, 1024), BF16),
        ],
        in_specs=[
            pl.BlockSpec((1024, 1024), lambda n: (0, 0)),
            pl.BlockSpec((4, 64, 256), lambda n: (0, 0, 0)),
            pl.BlockSpec((64, 1024), lambda n: (0, 0)),
            pl.BlockSpec(memory_space=pltpu.SMEM),
            hbm,
        ],
        out_specs=[
            pl.BlockSpec((1024, 512), lambda n: (0, n)),
            pl.BlockSpec((1, 512), lambda n: (0, n)),
            hbm,
        ],
        scratch_shapes=[pltpu.VMEM((1024, 128), F32), pltpu.VMEM((1024, 128), I32), dma(())],
        compiler_params=pltpu.CompilerParams(vmem_limit_bytes=48 * 2**20),
        name="enc_grads",
    )(cols, grad, idx_t, lax.axis_index("lat").reshape(1), dec_grad)
    return enc_grad, dec_grad, enc_bias_grad[0], bias_grad[0]


def solution(mesh):
    placed = (P("tok", None), P(), P("tok", "lat"), P("lat", "tok"), P("lat"), P("tok"))
    return jax.shard_map(
        local,
        mesh=mesh,
        in_specs=placed,
        out_specs=(P("tok", "lat"), P("lat", "tok"), P("lat"), P("tok")),
        check_vma=False,
    )
```

```python
import functools

import jax
import jax.numpy as jnp
from jax import lax
from jax.experimental import pallas as pl
from jax.experimental.pallas import tpu as pltpu
from jax.sharding import PartitionSpec as P

MESH = pl.DeviceIdType.MESH
F32, BF16, I32 = jnp.float32, jnp.bfloat16, jnp.int32
NT = (((1,), (1,)), ((), ()))
PLANE = tuple((dy, dx) for dy in range(4) for dx in range(4))
ORDER = (1, 3, 2)


def exchange(
    tokens, idx_t, enc, dec, enc_bias, dec_bias,
    cols_out, dec_grad_out, grad_out, bias_out,
    cols, enc_v, dec_v, key, key_t, picked, own_pre, pre_send, pre_recv,
    codes, code2, codes_t, dense, sib_send, sib_recv, part, rs_send, rs_recv,
    err, grad_part, grad_recv, dec_grad_v,
    sem_local, sem_a, sem_f, sem_b, sem_c, sem_s, sem_r, sem_g, sem_h, sem_d, sem_e, sem_o,
):
    z, lat = lax.axis_index("tok"), lax.axis_index("lat")
    y, x, core = lat // 8, (lat // 2) % 4, lat % 2
    other = 1 - core
    sibling = (z, lat + 1 - 2 * core)

    def along(offset):
        return lax.rem(z + offset, 4)

    def in_plane(dy, dx):
        return (z, lax.rem(y + dy, 4) * 8 + lax.rem(x + dx, 4) * 2 + core)

    def remote(src, dst, sems, index, device):
        return pltpu.make_async_remote_copy(
            src_ref=src, dst_ref=dst, send_sem=sems.at[0, index], recv_sem=sems.at[1, index],
            device_id=device, device_id_type=MESH,
        )

    barrier = pltpu.get_barrier_semaphore()
    peers = [(along(o), lat) for o in ORDER] + [sibling]
    peers += [in_plane(dy, dx) for dy, dx in PLANE if dy or dx]
    for peer in peers:
        pl.semaphore_signal(barrier, inc=1, device_id=peer, device_id_type=MESH)

    own_cols = pltpu.make_async_copy(
        tokens.at[:, pl.ds(pl.multiple_of(1024 * z, 1024), 1024)],
        cols.at[pl.ds(pl.multiple_of(256 * z, 256), 256)], sem_local.at[0])
    load_enc = pltpu.make_async_copy(enc, enc_v, sem_local.at[1])
    load_dec = pltpu.make_async_copy(dec, dec_v, sem_local.at[2])
    own_cols.start()
    load_enc.start()
    load_dec.start()

    pl.semaphore_wait(barrier, len(peers))

    half_rows = pl.ds(pl.multiple_of(128 * core, 128), 128)

    def block_half(block, which):
        return cols.at[pl.ds(pl.multiple_of(256 * block + 128 * which, 128), 128)]

    sends = {}
    for o in ORDER:
        to = along(o)
        sends[o] = remote(
            tokens.at[half_rows, pl.ds(pl.multiple_of(1024 * to, 1024), 1024)],
            block_half(z, core), sem_a, o, (to, lat))
        sends[o].start()

    band_t = lax.shift_right_logical(idx_t[...], 6) - 32 * lat
    key_t[...] = band_t
    odd = (lax.broadcasted_iota(I32, (128, 128), 1) >= 64).astype(I32)
    low = lax.broadcasted_iota(I32, (128, 128), 1) < 64
    for g in range(8):
        piece = band_t[:, 128 * g:128 * g + 128]
        key[128 * g:128 * g + 128, :] = jnp.concatenate([piece, piece], axis=0).T - odd

    own_cols.wait()
    load_enc.wait()

    def pre_block(block, with_bias):
        rows = pl.ds(pl.multiple_of(256 * block, 256), 256)
        picked[...] = jnp.zeros_like(picked)

        @pl.loop(0, 4)
        def _(n):
            base = pl.multiple_of(512 * n, 512)
            scores = jnp.dot(cols[rows, :], enc_v[:, pl.ds(base, 512)], preferred_element_type=F32)
            if with_bias:
                scores = scores + enc_bias[:, pl.ds(base, 512)]
            where = key[rows, :]
            total = picked[...]
            for j in range(4):
                total += jnp.where(where == 8 * n + 2 * j, scores[:, 128 * j:128 * j + 128], 0.0)
            picked[...] = total

        folded = picked[...]
        folded = folded + pltpu.roll(folded, 64, 1)
        return jnp.where(low, folded[:128], folded[128:])

    own_pre[...] = pre_block(z, True)
    forwards = {}
    returns = {}

    def forward(o):
        block = along(4 - o)
        sends[o].wait_recv()
        forwards[o] = remote(block_half(block, core), block_half(block, core), sem_f, o, sibling)
        forwards[o].start()

    def partial(o):
        block = along(4 - o)
        forwards[o].wait_recv()
        pre_send[o] = pre_block(block, False)
        returns[o] = remote(pre_send.at[o], pre_recv.at[o], sem_b, o, (block, lat))
        returns[o].start()

    forward(1)
    forward(3)
    partial(1)
    partial(3)
    forward(2)
    partial(2)

    store_cols = pltpu.make_async_copy(cols, cols_out, sem_local.at[3])
    store_cols.start()

    total = own_pre[...]
    for o in ORDER:
        returns[o].wait_recv()
        total = total + pre_recv[o]
    codes[z] = total.astype(BF16)
    spread_codes = {}
    for o in ORDER:
        spread_codes[o] = remote(codes.at[z], codes.at[z], sem_c, o, (along(o), lat))
        spread_codes[o].start()
    for o in ORDER:
        spread_codes[o].wait_recv()

    for block in range(4):
        packed = codes[block].astype(F32)
        turned = pltpu.roll(packed, 64, 1)
        for high in range(2):
            both = jnp.where(low, turned, packed) if high else jnp.where(low, packed, turned)
            g = 2 * block + high
            code2[128 * g:128 * g + 128, :] = both
            codes_t[:, 128 * g:128 * g + 128] = both.T[:64]

    load_dec.wait()

    def recon(half, chunk, out):
        for pos in range(2):
            dy = (1 + 2 * chunk + pos) % 4
            rows = pl.ds(pl.multiple_of(512 * half + 128 * lax.rem(y + dy, 4), 128), 128)
            where, values = key[rows, :], code2[rows, :]
            for j in range(16):
                dense[128 * pos:128 * pos + 128, 128 * j:128 * j + 128] = jnp.where(
                    where == 2 * j, values, 0.0).astype(BF16)

        @pl.loop(0, 2)
        def _(n):
            base = pl.ds(pl.multiple_of(512 * n, 512), 512)
            out[chunk, :, base] = jnp.dot(dense[...], dec_v[:, base], preferred_element_type=F32)

    to_sibling = {}

    def give(chunk):
        recon(other, chunk, sib_send)
        to_sibling[chunk] = remote(sib_send.at[chunk], sib_recv.at[chunk], sem_s, chunk, sibling)
        to_sibling[chunk].start()

    scatter = {}

    def finish(chunk):
        to_sibling[chunk].wait_recv()

        @pl.loop(0, 8)
        def _(i):
            rows = pl.ds(pl.multiple_of(32 * i, 32), 32)
            total = part[chunk, rows, :] + sib_recv[chunk, rows, :]
            part[chunk, rows, :] = total
            rs_send[chunk, rows, :] = total.astype(BF16)

        for pos in range(2):
            dy = (1 + 2 * chunk + pos) % 4
            for dx in range(4):
                if dy == 0 and dx == 0:
                    continue
                slot = 4 * dy + dx
                rows = pl.ds(pl.multiple_of(128 * pos + 32 * lax.rem(x + dx, 4), 32), 32)
                scatter[slot] = remote(rs_send.at[chunk, rows], rs_recv.at[slot], sem_r, slot, in_plane(dy, dx))
                scatter[slot].start()

    give(0)
    recon(core, 0, part)
    give(1)
    finish(0)
    recon(core, 1, part)
    finish(1)

    mine = pl.ds(pl.multiple_of(512 * core + 128 * y + 32 * x, 32), 32)
    full = part[1, pl.ds(pl.multiple_of(128 + 32 * x, 32), 32), :]
    full = full + dec_bias[...] - cols[mine, :].astype(F32)
    for slot in range(1, 16):
        scatter[slot].wait_recv()
        full = full + rs_recv[slot].astype(F32)
    err[mine, :] = full.astype(BF16)

    gather = {}
    for dy, dx in PLANE:
        if dy or dx:
            slot = 4 * dy + dx
            gather[slot] = remote(err.at[mine], err.at[mine], sem_g, slot, in_plane(dy, dx))
            gather[slot].start()
    across = {}
    for dy in range(4):
        for dx in range(4):
            if dy or dx:
                gather[4 * dy + dx].wait_recv()
        rows = pl.ds(pl.multiple_of(512 * core + 128 * lax.rem(y + 4 - dy, 4), 128), 128)
        across[dy] = remote(err.at[rows], err.at[rows], sem_h, dy, sibling)
        across[dy].start()

    def code_grad(block):
        rows = pl.ds(pl.multiple_of(256 * block, 256), 256)
        grad_part[block] = jnp.zeros((64, 256), F32)

        @pl.loop(0, 4)
        def _(n):
            lats = pl.ds(pl.multiple_of(512 * n, 512), 512)
            scores = lax.dot_general(dec_v[lats, :], err[rows, :], NT, preferred_element_type=F32)
            where = key_t[:, rows]
            total = grad_part[block]
            for b in range(8):
                total += jnp.where(where == 8 * n + b, scores[64 * b:64 * b + 64, :], 0.0)
            grad_part[block] = total

    code_grad(2 * core)
    code_grad(2 * core + 1)
    for dy in range(4):
        across[dy].wait_recv()
    code_grad(2 * other)
    code_grad(2 * other + 1)

    grads = {}
    for o in ORDER:
        to = along(o)
        grads[o] = remote(grad_part.at[to], grad_recv.at[o], sem_d, o, (to, lat))
        grads[o].start()

    bias_out[...] = jnp.dot(jnp.ones((16, 1024), BF16), err[...], preferred_element_type=F32)[:8]

    def dec_rows(n):
        return pl.ds(pl.multiple_of(256 * n, 256), 256)

    def dec_grads(first, last):
        @pl.loop(first, last)
        def _(n):
            where, values = key_t[...], codes_t[...]
            wide = jnp.concatenate(
                [jnp.where(where == 4 * n + b, values, 0.0).astype(BF16) for b in range(4)], axis=0)
            dec_grad_v[dec_rows(n), :] = jnp.dot(wide, err[...], preferred_element_type=F32).astype(BF16)
            pltpu.make_async_copy(dec_grad_v.at[dec_rows(n)], dec_grad_out.at[dec_rows(n)], sem_o.at[n]).start()

    dec_grads(0, 4)
    total = grad_part[z]
    for o in ORDER:
        grads[o].wait_recv()
        total = total + grad_recv[o]
    grad_out[z] = total
    shares = {}
    for o in ORDER:
        shares[o] = remote(grad_out.at[z], grad_out.at[z], sem_e, o, (along(o), lat))
        shares[o].start()
    dec_grads(4, 8)

    for o in ORDER:
        shares[o].wait()
        for group in (sends, forwards, returns, spread_codes, grads):
            group[o].wait_send()
    for group in (to_sibling, scatter, gather, across):
        for copy in group.values():
            copy.wait_send()
    store_cols.wait()

    @pl.loop(0, 8)
    def _(n):
        pltpu.make_async_copy(dec_grad_v.at[dec_rows(n)], dec_grad_out.at[dec_rows(n)], sem_o.at[n]).wait()


def enc_grads(cols, grad, idx_t, lat_ref, dec_in, enc_out, enc_bias_out, dec_out, grad2, key):
    n = pl.program_id(0)

    @pl.when(n == 0)
    def _():
        odd = (lax.broadcasted_iota(I32, (128, 128), 1) >= 64).astype(I32)
        for g in range(8):
            piece = lax.shift_right_logical(idx_t[:, 128 * g:128 * g + 128], 6) - 32 * lat_ref[0]
            key[128 * g:128 * g + 128, :] = jnp.concatenate([piece, piece], axis=0).T - odd
            piece = grad[g // 2, :, 128 * (g % 2):128 * (g % 2) + 128]
            grad2[128 * g:128 * g + 128, :] = jnp.concatenate([piece, piece], axis=0).T

    where, values = key[...], grad2[...]
    wide = [jnp.where(where == 8 * n + 2 * j, values, 0.0) for j in range(4)]
    for j in range(4):
        enc_bias_out[:, 128 * j:128 * j + 128] = jnp.sum(wide[j], axis=0, keepdims=True)
    wide = jnp.concatenate([w.astype(BF16) for w in wide], axis=1)
    enc_out[...] = lax.dot_general(
        cols[...], wide, (((0,), (0,)), ((), ())), preferred_element_type=F32).astype(BF16)
    dec_out[...] = dec_in[...]


def local(tokens, indices, enc_weight, dec_weight, enc_bias, dec_bias):
    idx_t = indices.T
    vmem = pl.BlockSpec(memory_space=pltpu.VMEM)
    hbm = pl.BlockSpec(memory_space=pl.ANY)
    dma = pltpu.SemaphoreType.DMA
    cols, dec_grad, grad, bias_grad = pl.pallas_call(
        exchange,
        out_shape=[
            jax.ShapeDtypeStruct((1024, 1024), BF16),
            jax.ShapeDtypeStruct((2048, 1024), BF16),
            jax.ShapeDtypeStruct((4, 64, 256), F32),
            jax.ShapeDtypeStruct((8, 1024), F32),
        ],
        in_specs=[hbm, vmem, hbm, hbm, vmem, vmem],
        out_specs=[hbm, hbm, vmem, vmem],
        scratch_shapes=[
            pltpu.VMEM((1024, 1024), BF16),
            pltpu.VMEM((1024, 2048), BF16),
            pltpu.VMEM((2048, 1024), BF16),
            pltpu.VMEM((1024, 128), I32),
            pltpu.VMEM((64, 1024), I32),
            pltpu.VMEM((256, 128), F32),
            pltpu.VMEM((128, 128), F32),
            pltpu.VMEM((4, 128, 128), F32),
            pltpu.VMEM((4, 128, 128), F32),
            pltpu.VMEM((4, 128, 128), BF16),
            pltpu.VMEM((1024, 128), F32),
            pltpu.VMEM((64, 1024), F32),
            pltpu.VMEM((256, 2048), BF16),
            pltpu.VMEM((2, 256, 1024), F32),
            pltpu.VMEM((2, 256, 1024), F32),
            pltpu.VMEM((2, 256, 1024), F32),
            pltpu.VMEM((2, 256, 1024), BF16),
            pltpu.VMEM((16, 32, 1024), BF16),
            pltpu.VMEM((1024, 1024), BF16),
            pltpu.VMEM((4, 64, 256), F32),
            pltpu.VMEM((4, 64, 256), F32),
            pltpu.VMEM((2048, 1024), BF16),
            dma((4,)), dma((2, 4)), dma((2, 4)), dma((2, 4)), dma((2, 4)), dma((2, 2)),
            dma((2, 16)), dma((2, 16)), dma((2, 4)), dma((2, 4)), dma((2, 4)), dma((8,)),
        ],
        compiler_params=pltpu.CompilerParams(
            collective_id=0, has_side_effects=True, vmem_limit_bytes=48 * 2**20),
        name="exchange",
    )(tokens, idx_t, enc_weight, dec_weight, enc_bias[None, :], dec_bias[None, :])

    enc_grad, enc_bias_grad, dec_grad = pl.pallas_call(
        enc_grads,
        grid=(4,),
        out_shape=[
            jax.ShapeDtypeStruct((1024, 2048), BF16),
            jax.ShapeDtypeStruct((1, 2048), F32),
            jax.ShapeDtypeStruct((2048, 1024), BF16),
        ],
        in_specs=[
            pl.BlockSpec((1024, 1024), lambda n: (0, 0)),
            pl.BlockSpec((4, 64, 256), lambda n: (0, 0, 0)),
            pl.BlockSpec((64, 1024), lambda n: (0, 0)),
            pl.BlockSpec(memory_space=pltpu.SMEM),
            pl.BlockSpec((512, 1024), lambda n: (n, 0)),
        ],
        out_specs=[
            pl.BlockSpec((1024, 512), lambda n: (0, n)),
            pl.BlockSpec((1, 512), lambda n: (0, n)),
            pl.BlockSpec((512, 1024), lambda n: (n, 0)),
        ],
        scratch_shapes=[pltpu.VMEM((1024, 128), F32), pltpu.VMEM((1024, 128), I32)],
        compiler_params=pltpu.CompilerParams(vmem_limit_bytes=48 * 2**20),
        name="enc_grads",
    )(cols, grad, idx_t, lax.axis_index("lat").reshape(1), dec_grad)
    return enc_grad, dec_grad, enc_bias_grad[0], bias_grad[0]


def solution(mesh):
    placed = (P("tok", None), P(), P("tok", "lat"), P("lat", "tok"), P("lat"), P("tok"))
    return jax.shard_map(
        local,
        mesh=mesh,
        in_specs=placed,
        out_specs=(P("tok", "lat"), P("lat", "tok"), P("lat"), P("tok")),
        check_vma=False,
    )
```

```python
import jax
import jax.numpy as jnp
from jax import lax
from jax.experimental import pallas as pl
from jax.experimental.pallas import tpu as pltpu
from jax.sharding import PartitionSpec as P

MESH = pl.DeviceIdType.MESH
F32, BF16, I32 = jnp.float32, jnp.bfloat16, jnp.int32
NT = (((1,), (1,)), ((), ()))
PLANE = tuple((dy, dx) for dy in range(4) for dx in range(4))
ORDER = (1, 3, 2)


def exchange(
    tokens, idx_in, enc, dec, enc_bias, dec_bias,
    cols_out, dec_grad_out, grad_out, bias_out,
    idx_t, bias_e, bias_d, cols, enc2, dec2, key, key_t, picked, own_pre, pre_send, pre_recv,
    codes, dense, part, rs_send, rs_recv, err, grad_part, grad_recv, dec_grad_v,
    sem_local, sem_a, sem_w, sem_f, sem_b, sem_c, sem_k, sem_r, sem_g, sem_h, sem_d, sem_e, sem_o,
):
    z, lat = lax.axis_index("tok"), lax.axis_index("lat")
    y, x, core = lat // 8, (lat // 2) % 4, lat % 2
    other = 1 - core
    sib_lat = lat + 1 - 2 * core
    sibling = (z, sib_lat)

    def along(offset):
        return lax.rem(z + offset, 4)

    def in_plane(dy, dx):
        return (z, lax.rem(y + dy, 4) * 8 + lax.rem(x + dx, 4) * 2 + core)

    def remote(src, dst, sems, index, device):
        return pltpu.make_async_remote_copy(
            src_ref=src, dst_ref=dst, send_sem=sems.at[0, index], recv_sem=sems.at[1, index],
            device_id=device, device_id_type=MESH,
        )

    barrier = pltpu.get_barrier_semaphore()
    peers = [(along(o), lat) for o in ORDER] + [sibling]
    peers += [(along(o), sib_lat) for o in ORDER]
    peers += [in_plane(dy, dx) for dy, dx in PLANE if dy or dx]
    for peer in peers:
        pl.semaphore_signal(barrier, inc=1, device_id=peer, device_id_type=MESH)

    enc_rows = pl.ds(pl.multiple_of(1024 * core, 1024), 1024)
    dec_rows = pl.ds(pl.multiple_of(2048 * core, 2048), 2048)
    loads = [
        pltpu.make_async_copy(
            tokens.at[:, pl.ds(pl.multiple_of(1024 * z, 1024), 1024)],
            cols.at[pl.ds(pl.multiple_of(256 * z, 256), 256)], sem_local.at[0]),
        pltpu.make_async_copy(idx_in, idx_t, sem_local.at[1]),
        pltpu.make_async_copy(enc_bias, bias_e.at[core], sem_local.at[2]),
        pltpu.make_async_copy(enc, enc2.at[enc_rows], sem_local.at[3]),
        pltpu.make_async_copy(dec_bias, bias_d, sem_local.at[4]),
        pltpu.make_async_copy(dec, dec2.at[dec_rows], sem_local.at[5]),
    ]
    for copy in loads:
        copy.start()

    pl.semaphore_wait(barrier, len(peers))

    def half(block, which):
        return pl.ds(pl.multiple_of(256 * block + 128 * which, 128), 128)

    sends = {}
    for o in ORDER:
        to = along(o)
        sends[o] = remote(
            tokens.at[pl.ds(pl.multiple_of(128 * core, 128), 128), pl.ds(pl.multiple_of(1024 * to, 1024), 1024)],
            cols.at[half(z, core)], sem_a, o, (to, lat))
        sends[o].start()
    give_bias = remote(enc_bias, bias_e.at[core], sem_w, 0, sibling)
    give_enc = remote(enc, enc2.at[enc_rows], sem_w, 1, sibling)
    give_dec = remote(dec, dec2.at[dec_rows], sem_w, 2, sibling)
    give_bias.start()
    give_enc.start()

    loads[1].wait()
    odd = (lax.broadcasted_iota(I32, (128, 128), 1) >= 64).astype(I32)
    for g in range(4):
        for h in range(2):
            at = 256 * g + 128 * h
            band = lax.shift_right_logical(idx_t[:, at:at + 128], 6) - 64 * (lat // 2)
            key_t[:, 512 * h + 128 * g:512 * h + 128 * g + 128] = band
        band = lax.shift_right_logical(idx_t[:, half(g, core)], 6) - 64 * (lat // 2)
        key[g] = jnp.concatenate([band, band], axis=0).T - odd

    def pick(blocks, which, bias_first):
        rows = jnp.concatenate([cols[half(b, core), :] for b in blocks], axis=0) if len(blocks) > 1 else cols[half(blocks[0], core), :]
        weights = pl.ds(pl.multiple_of(1024 * which, 1024), 1024)

        @pl.loop(0, 4)
        def _(n):
            base = pl.multiple_of(512 * n, 512)
            scores = jnp.dot(rows, enc2[weights, pl.ds(base, 512)], preferred_element_type=F32)
            if bias_first:
                scores = scores + bias_e[which, :, pl.ds(base, 512)]
            for i, b in enumerate(blocks):
                where = key[b]
                total = picked[b]
                for j in range(4):
                    total += jnp.where(
                        where == 32 * which + 8 * n + 2 * j,
                        scores[128 * i:128 * i + 128, 128 * j:128 * j + 128], 0.0)
                picked[b] = total

    def folded(block):
        turned = picked[block].T
        return turned[:64] + turned[64:]

    picked[...] = jnp.zeros_like(picked)
    loads[0].wait()
    loads[2].wait()
    loads[3].wait()
    pick([z], core, True)

    returns = {}
    forwards = {}

    def forward(o):
        rows = half(along(4 - o), core)
        forwards[o] = remote(cols.at[rows], cols.at[rows], sem_f, o, sibling)
        forwards[o].start()

    def give_back(o):
        pre_send[o] = folded(along(4 - o))
        returns[o] = remote(pre_send.at[o], pre_recv.at[o], sem_b, o, (along(4 - o), lat))
        returns[o].start()

    give_bias.wait_recv()
    give_enc.wait_recv()
    give_enc.wait_send()
    give_dec.start()
    pick([z], other, True)
    own_pre[...] = folded(z)
    sends[1].wait_recv()
    sends[3].wait_recv()
    pair = [along(3), along(1)]
    pick(pair, core, False)
    pick(pair, other, False)
    give_back(1)
    give_back(3)
    sends[2].wait_recv()
    last = [along(2)]
    pick(last, core, False)
    pick(last, other, False)
    give_back(2)
    for o in ORDER:
        forward(o)

    total = own_pre[...]
    for o in ORDER:
        returns[o].wait_recv()
        total = total + pre_recv[o]
    codes[core, z] = total.astype(BF16)
    shared = {}
    for o in ORDER:
        shared[o] = remote(codes.at[core, z], codes.at[core, z], sem_c, o, (along(o), lat))
        shared[o].start()
    for copy in loads[4:]:
        copy.wait()
    give_dec.wait_recv()
    for o in ORDER:
        shared[o].wait_recv()
    swap_codes = remote(codes.at[core], codes.at[core], sem_k, 0, sibling)
    swap_codes.start()

    scatter = {}

    def recon(chunk):
        groups = [lax.rem(y + (1 + 2 * chunk + pos) % 4, 4) for pos in range(2)]
        for pos in range(2):
            turned = codes[core, groups[pos]].astype(F32)
            values = jnp.concatenate([turned, turned], axis=0).T
            where = key[groups[pos]]
            for j in range(32):
                dense[128 * pos:128 * pos + 128, 128 * j:128 * j + 128] = jnp.where(
                    where == 2 * j, values, 0.0).astype(BF16)

        @pl.loop(0, 2)
        def _(n):
            base = pl.ds(pl.multiple_of(512 * n, 512), 512)
            out = jnp.dot(dense[...], dec2[:, base], preferred_element_type=F32)
            if chunk == 1:
                part[:, base] = out[128:]
            rs_send[chunk, :, base] = out.astype(BF16)

        for pos in range(2):
            dy = (1 + 2 * chunk + pos) % 4
            for dx in range(4):
                if dy == 0 and dx == 0:
                    continue
                slot = 4 * dy + dx
                rows = pl.ds(pl.multiple_of(128 * pos + 32 * lax.rem(x + dx, 4), 32), 32)
                scatter[slot] = remote(rs_send.at[chunk, rows], rs_recv.at[slot], sem_r, slot, in_plane(dy, dx))
                scatter[slot].start()

    recon(0)
    recon(1)

    mine = pl.ds(pl.multiple_of(32 * x, 32), 32)
    full = part[mine, :] + bias_d[...]
    full = full - cols[pl.ds(pl.multiple_of(256 * y + 128 * core + 32 * x, 32), 32), :].astype(F32)
    for slot in range(1, 16):
        scatter[slot].wait_recv()
        full = full + rs_recv[slot].astype(F32)
    err[core, y, mine, :] = full.astype(BF16)

    gather = {}
    for dy, dx in PLANE:
        if dy or dx:
            slot = 4 * dy + dx
            gather[slot] = remote(
                err.at[core, y, mine], err.at[core, y, mine], sem_g, slot, in_plane(dy, dx))
            gather[slot].start()

    across = {}

    def code_grad(dys):
        groups = []
        for dy in dys:
            for dx in range(4):
                if dy or dx:
                    gather[4 * dy + dx].wait_recv()
            group = lax.rem(y + 4 - dy, 4)
            across[dy] = remote(err.at[core, group], err.at[core, group], sem_h, dy, sibling)
            across[dy].start()
            groups.append(group)
        rows = jnp.concatenate([err[core, g] for g in groups], axis=0)
        for g in groups:
            grad_part[g] = jnp.zeros((64, 128), F32)

        @pl.loop(0, 8)
        def _(n):
            lats = pl.ds(pl.multiple_of(512 * n, 512), 512)
            scores = lax.dot_general(dec2[lats, :], rows, NT, preferred_element_type=F32)
            for i, g in enumerate(groups):
                where = key_t[:, pl.ds(pl.multiple_of(512 * core + 128 * g, 128), 128)]
                total = grad_part[g]
                for b in range(8):
                    total += jnp.where(
                        where == 8 * n + b, scores[64 * b:64 * b + 64, 128 * i:128 * i + 128], 0.0)
                grad_part[g] = total

    code_grad((0, 1))
    code_grad((2, 3))

    grads = {}
    for o in ORDER:
        to = along(o)
        grads[o] = remote(grad_part.at[to], grad_recv.at[o], sem_d, o, (to, lat))
        grads[o].start()

    swap_codes.wait_recv()
    for dy in range(4):
        across[dy].wait_recv()

    def tile(n):
        return pl.ds(pl.multiple_of(256 * n, 256), 256)

    def dec_grads(first, last):
        values = jnp.concatenate(
            [codes[h, g].astype(F32) for h in range(2) for g in range(4)], axis=1)
        errors = err[...].reshape(1024, 1024)

        @pl.loop(first, last)
        def _(n):
            where = key_t[...]
            wide = jnp.concatenate(
                [jnp.where(where == 32 * core + 4 * n + b, values, 0.0).astype(BF16) for b in range(4)], axis=0)
            dec_grad_v[tile(n), :] = jnp.dot(wide, errors, preferred_element_type=F32).astype(BF16)
            pltpu.make_async_copy(dec_grad_v.at[tile(n)], dec_grad_out.at[tile(n)], sem_o.at[n]).start()

    for o in ORDER:
        forwards[o].wait_recv()
    store_cols = pltpu.make_async_copy(cols, cols_out, sem_local.at[6])
    store_cols.start()
    dec_grads(0, 4)
    total = grad_part[z]
    for o in ORDER:
        grads[o].wait_recv()
        total = total + grad_recv[o]
    grad_out[core, z] = total
    shares = []
    for o in (0,) + ORDER:
        if o:
            shares.append(remote(grad_out.at[core, z], grad_out.at[core, z], sem_e, o, (along(o), lat)))
            shares[-1].start()
        shares.append(remote(grad_out.at[core, z], grad_out.at[core, z], sem_e, 4 + o, (along(o), sib_lat)))
        shares[-1].start()
    dec_grads(4, 8)
    bias_out[...] = jnp.dot(
        jnp.ones((16, 1024), BF16), err[...].reshape(1024, 1024), preferred_element_type=F32)[:1]

    for copy in shares:
        copy.wait()
    for o in ORDER:
        for group in (sends, forwards, returns, shared, grads):
            group[o].wait_send()
    for copy in [give_bias, give_dec, swap_codes] + list(scatter.values()) + list(gather.values()) + list(across.values()):
        copy.wait_send()
    store_cols.wait()

    @pl.loop(0, 8)
    def _(n):
        pltpu.make_async_copy(dec_grad_v.at[tile(n)], dec_grad_out.at[tile(n)], sem_o.at[n]).wait()


def enc_grads(cols, grad, idx_t, lat_ref, dec_in, enc_out, enc_bias_out, dec_out, grad2, key):
    n = pl.program_id(0)

    @pl.when(n == 0)
    def _():
        odd = (lax.broadcasted_iota(I32, (128, 128), 1) >= 64).astype(I32)
        for g in range(8):
            piece = lax.shift_right_logical(idx_t[:, 128 * g:128 * g + 128], 6) - 32 * lat_ref[0]
            key[128 * g:128 * g + 128, :] = jnp.concatenate([piece, piece], axis=0).T - odd
            piece = grad[g % 2, g // 2]
            grad2[128 * g:128 * g + 128, :] = jnp.concatenate([piece, piece], axis=0).T

    where, values = key[...], grad2[...]
    wide = [jnp.where(where == 8 * n + 2 * j, values, 0.0) for j in range(4)]
    for j in range(4):
        enc_bias_out[:, 128 * j:128 * j + 128] = jnp.sum(wide[j], axis=0, keepdims=True)
    wide = jnp.concatenate([w.astype(BF16) for w in wide], axis=1)
    enc_out[...] = lax.dot_general(
        cols[...], wide, (((0,), (0,)), ((), ())), preferred_element_type=F32).astype(BF16)
    dec_out[...] = dec_in[...]


def local(tokens, indices, enc_weight, dec_weight, enc_bias, dec_bias):
    idx_t = indices.T
    vmem = pl.BlockSpec(memory_space=pltpu.VMEM)
    hbm = pl.BlockSpec(memory_space=pl.ANY)
    dma = pltpu.SemaphoreType.DMA
    cols, dec_grad, grad, bias_grad = pl.pallas_call(
        exchange,
        out_shape=[
            jax.ShapeDtypeStruct((1024, 1024), BF16),
            jax.ShapeDtypeStruct((2048, 1024), BF16),
            jax.ShapeDtypeStruct((2, 4, 64, 128), F32),
            jax.ShapeDtypeStruct((1, 1024), F32),
        ],
        in_specs=[hbm] * 6,
        out_specs=[hbm, hbm, vmem, vmem],
        scratch_shapes=[
            pltpu.VMEM((64, 1024), I32),
            pltpu.VMEM((2, 1, 2048), F32),
            pltpu.VMEM((1, 1024), F32),
            pltpu.VMEM((1024, 1024), BF16),
            pltpu.VMEM((2048, 2048), BF16),
            pltpu.VMEM((4096, 1024), BF16),
            pltpu.VMEM((4, 128, 128), I32),
            pltpu.VMEM((64, 1024), I32),
            pltpu.VMEM((4, 128, 128), F32),
            pltpu.VMEM((64, 128), F32),
            pltpu.VMEM((4, 64, 128), F32),
            pltpu.VMEM((4, 64, 128), F32),
            pltpu.VMEM((2, 4, 64, 128), BF16),
            pltpu.VMEM((256, 4096), BF16),
            pltpu.VMEM((128, 1024), F32),
            pltpu.VMEM((2, 256, 1024), BF16),
            pltpu.VMEM((16, 32, 1024), BF16),
            pltpu.VMEM((2, 4, 128, 1024), BF16),
            pltpu.VMEM((4, 64, 128), F32),
            pltpu.VMEM((4, 64, 128), F32),
            pltpu.VMEM((2048, 1024), BF16),
            dma((7,)), dma((2, 4)), dma((2, 3)), dma((2, 4)), dma((2, 4)), dma((2, 4)), dma((2, 1)),
            dma((2, 16)), dma((2, 16)), dma((2, 4)), dma((2, 4)), dma((2, 8)), dma((8,)),
        ],
        compiler_params=pltpu.CompilerParams(
            collective_id=0, has_side_effects=True, vmem_limit_bytes=58 * 2**20),
        name="exchange",
    )(tokens, idx_t, enc_weight, dec_weight, enc_bias[None, :], dec_bias[None, :])

    enc_grad, enc_bias_grad, dec_grad = pl.pallas_call(
        enc_grads,
        grid=(4,),
        out_shape=[
            jax.ShapeDtypeStruct((1024, 2048), BF16),
            jax.ShapeDtypeStruct((1, 2048), F32),
            jax.ShapeDtypeStruct((2048, 1024), BF16),
        ],
        in_specs=[
            pl.BlockSpec((1024, 1024), lambda n: (0, 0)),
            pl.BlockSpec((2, 4, 64, 128), lambda n: (0, 0, 0, 0)),
            pl.BlockSpec((64, 1024), lambda n: (0, 0)),
            pl.BlockSpec(memory_space=pltpu.SMEM),
            pl.BlockSpec((512, 1024), lambda n: (n, 0)),
        ],
        out_specs=[
            pl.BlockSpec((1024, 512), lambda n: (0, n)),
            pl.BlockSpec((1, 512), lambda n: (0, n)),
            pl.BlockSpec((512, 1024), lambda n: (n, 0)),
        ],
        scratch_shapes=[pltpu.VMEM((1024, 128), F32), pltpu.VMEM((1024, 128), I32)],
        compiler_params=pltpu.CompilerParams(vmem_limit_bytes=58 * 2**20),
        name="enc_grads",
    )(cols, grad, idx_t, lax.axis_index("lat").reshape(1), dec_grad)
    return enc_grad, dec_grad, enc_bias_grad[0], bias_grad[0]


def solution(mesh):
    placed = (P("tok", None), P(), P("tok", "lat"), P("lat", "tok"), P("lat"), P("tok"))
    return jax.shard_map(
        local,
        mesh=mesh,
        in_specs=placed,
        out_specs=(P("tok", "lat"), P("lat", "tok"), P("lat"), P("tok")),
        check_vma=False,
    )
```

```python
import jax
import jax.numpy as jnp
from jax import lax
from jax.experimental import pallas as pl
from jax.experimental.pallas import tpu as pltpu
from jax.sharding import PartitionSpec as P

MESH = pl.DeviceIdType.MESH
F32, BF16, I32 = jnp.float32, jnp.bfloat16, jnp.int32
NT = (((1,), (1,)), ((), ()))
PLANE = tuple((dy, dx) for dy in range(4) for dx in range(4))
ORDER = (1, 3, 2)


def exchange(
    tokens, idx_in, enc, dec, enc_bias, dec_bias,
    cols_out, dec_grad_out, grad_out, bias_out,
    idx_t, bias_e, bias_d, cols, enc2, dec2, key, key_t, picked, own_pre, pre_send, pre_recv,
    codes, dense, cols_t, rs_send, rs_recv, err, grad_part, grad_recv, dec_grad_v,
    sem_local, sem_a, sem_w, sem_f, sem_b, sem_c, sem_k, sem_r, sem_g, sem_h, sem_d, sem_e, sem_o,
):
    z, lat = lax.axis_index("tok"), lax.axis_index("lat")
    y, x, core = lat // 8, (lat // 2) % 4, lat % 2
    other = 1 - core
    sib_lat = lat + 1 - 2 * core
    sibling = (z, sib_lat)

    def along(offset):
        return lax.rem(z + offset, 4)

    def in_plane(dy, dx):
        return (z, lax.rem(y + dy, 4) * 8 + lax.rem(x + dx, 4) * 2 + core)

    def remote(src, dst, sems, index, device):
        return pltpu.make_async_remote_copy(
            src_ref=src, dst_ref=dst, send_sem=sems.at[0, index], recv_sem=sems.at[1, index],
            device_id=device, device_id_type=MESH,
        )

    barrier = pltpu.get_barrier_semaphore()
    peers = [(along(o), lat) for o in ORDER] + [sibling]
    peers += [(along(o), sib_lat) for o in ORDER]
    peers += [in_plane(dy, dx) for dy, dx in PLANE if dy or dx]
    for peer in peers:
        pl.semaphore_signal(barrier, inc=1, device_id=peer, device_id_type=MESH)

    enc_rows = pl.ds(pl.multiple_of(1024 * core, 1024), 1024)
    dec_rows = pl.ds(pl.multiple_of(2048 * core, 2048), 2048)
    loads = [
        pltpu.make_async_copy(
            tokens.at[:, pl.ds(pl.multiple_of(1024 * z, 1024), 1024)],
            cols.at[pl.ds(pl.multiple_of(256 * z, 256), 256)], sem_local.at[0]),
        pltpu.make_async_copy(idx_in, idx_t, sem_local.at[1]),
        pltpu.make_async_copy(enc_bias, bias_e.at[core], sem_local.at[2]),
        pltpu.make_async_copy(enc, enc2.at[enc_rows], sem_local.at[3]),
        pltpu.make_async_copy(dec_bias, bias_d, sem_local.at[4]),
        pltpu.make_async_copy(dec, dec2.at[dec_rows], sem_local.at[5]),
    ]
    for copy in loads:
        copy.start()

    pl.semaphore_wait(barrier, len(peers))

    def half(block, which):
        return pl.ds(pl.multiple_of(256 * block + 128 * which, 128), 128)

    sends = {}
    for o in ORDER:
        to = along(o)
        sends[o] = remote(
            tokens.at[pl.ds(pl.multiple_of(128 * core, 128), 128), pl.ds(pl.multiple_of(1024 * to, 1024), 1024)],
            cols.at[half(z, core)], sem_a, o, (to, lat))
        if o != 2:
            sends[o].start()
    give_bias = remote(enc_bias, bias_e.at[core], sem_w, 0, sibling)
    give_enc = remote(enc, enc2.at[enc_rows], sem_w, 1, sibling)
    give_dec = remote(dec, dec2.at[dec_rows], sem_w, 2, sibling)
    give_bias.start()
    give_enc.start()

    loads[1].wait()
    odd = (lax.broadcasted_iota(I32, (128, 128), 1) >= 64).astype(I32)
    for g in range(4):
        for h in range(2):
            at = 256 * g + 128 * h
            band = lax.shift_right_logical(idx_t[:, at:at + 128], 6) - 64 * (lat // 2)
            key_t[:, 512 * h + 128 * g:512 * h + 128 * g + 128] = band
        band = lax.shift_right_logical(idx_t[:, half(g, core)], 6) - 64 * (lat // 2)
        key[g] = jnp.concatenate([band, band], axis=0).T - odd

    def pick(blocks, which, bias_first):
        rows = jnp.concatenate([cols[half(b, core), :] for b in blocks], axis=0) if len(blocks) > 1 else cols[half(blocks[0], core), :]
        weights = pl.ds(pl.multiple_of(1024 * which, 1024), 1024)

        @pl.loop(0, 4, unroll=True)
        def _(n):
            base = pl.multiple_of(512 * n, 512)
            scores = jnp.dot(rows, enc2[weights, pl.ds(base, 512)], preferred_element_type=F32)
            if bias_first:
                scores = scores + bias_e[which, :, pl.ds(base, 512)]
            for i, b in enumerate(blocks):
                where = key[b]
                total = picked[b]
                for j in range(4):
                    total += jnp.where(
                        where == 32 * which + 8 * n + 2 * j,
                        scores[128 * i:128 * i + 128, 128 * j:128 * j + 128], 0.0)
                picked[b] = total

    def folded(block):
        turned = picked[block].T
        return turned[:64] + turned[64:]

    picked[...] = jnp.zeros_like(picked)
    loads[0].wait()
    loads[2].wait()
    loads[3].wait()
    pick([z], core, True)

    returns = {}
    forwards = {}

    def forward(o):
        rows = half(along(4 - o), core)
        forwards[o] = remote(cols.at[rows], cols.at[rows], sem_f, o, sibling)
        forwards[o].start()

    def give_back(o):
        pre_send[o] = folded(along(4 - o))
        returns[o] = remote(pre_send.at[o], pre_recv.at[o], sem_b, o, (along(4 - o), lat))
        returns[o].start()

    sends[1].wait_send()
    sends[3].wait_send()
    sends[2].start()
    sends[1].wait_recv()
    sends[3].wait_recv()
    pair = [along(3), along(1)]
    pick(pair, core, False)
    give_bias.wait_recv()
    give_enc.wait()
    give_dec.start()
    pick(pair, other, False)
    give_back(1)
    give_back(3)
    pick([z], other, True)
    own_pre[...] = folded(z)
    sends[2].wait_recv()
    last = [along(2)]
    pick(last, core, False)
    pick(last, other, False)
    give_back(2)
    for o in ORDER:
        forward(o)

    total = own_pre[...]
    for o in ORDER:
        returns[o].wait_recv()
        total = total + pre_recv[o]
    codes[core, z] = total.astype(BF16)
    shared = {}
    for o in ORDER:
        shared[o] = remote(codes.at[core, z], codes.at[core, z], sem_c, o, (along(o), lat))
        shared[o].start()
    for copy in loads[4:]:
        copy.wait()
    give_dec.wait_recv()
    for o in ORDER:
        shared[o].wait_recv()
    swap_codes = remote(codes.at[core], codes.at[core], sem_k, 0, sibling)
    swap_codes.start()

    spot = 4 * y + x
    scatter, gather, across = {}, {}, {}

    def share(chunk, place):
        return pl.ds(pl.multiple_of(256 * chunk + 16 * place, 16), 16)

    def partners(chunk):
        for slot in range(1, 16):
            dy, dx = PLANE[slot]
            place = 4 * lax.rem(y + dy, 4) + lax.rem(x + dx, 4)
            yield 16 * chunk + slot, place, in_plane(dy, dx)

    def recon(chunk):
        for pos in range(2):
            turned = codes[core, 2 * chunk + pos].astype(F32)
            values = jnp.concatenate([turned, turned], axis=0).T
            where = key[2 * chunk + pos]
            for j in range(32):
                dense[128 * pos:128 * pos + 128, 128 * j:128 * j + 128] = jnp.where(
                    where == 2 * j, values, 0.0).astype(BF16)

        @pl.loop(0, 2, unroll=True)
        def _(n):
            base = pl.ds(pl.multiple_of(512 * n, 512), 512)
            rs_send[256 * chunk:256 * chunk + 256, base] = jnp.dot(
                dense[...], dec2[:, base], preferred_element_type=F32).astype(BF16)

        for slot, place, device in partners(chunk):
            scatter[slot] = remote(rs_send.at[share(chunk, place)], rs_recv.at[slot], sem_r, slot, device)
            scatter[slot].start()

    def error(chunk):
        mine = share(chunk, spot)
        rows = pl.ds(pl.multiple_of(512 * chunk + 256 * (spot // 8) + 128 * core + 16 * lax.rem(spot, 8), 16), 16)
        full = rs_send[mine, :].astype(F32) + bias_d[...]
        full = full - cols[rows, :].astype(F32)
        for slot in range(16 * chunk + 1, 16 * chunk + 16):
            scatter[slot].wait_recv()
            full = full + rs_recv[slot].astype(F32)
        err[core, mine, :] = full.astype(BF16)
        for slot, _, device in partners(chunk):
            gather[slot] = remote(err.at[core, mine], err.at[core, mine], sem_g, slot, device)
            gather[slot].start()

    def code_grad(chunk):
        for slot in range(16 * chunk + 1, 16 * chunk + 16):
            gather[slot].wait_recv()
        rows = slice(256 * chunk, 256 * chunk + 256)
        across[chunk] = remote(err.at[core, rows], err.at[core, rows], sem_h, chunk, sibling)
        across[chunk].start()
        errors = err[core, rows, :]
        groups = (2 * chunk, 2 * chunk + 1)
        for g in groups:
            grad_part[g] = jnp.zeros((64, 128), F32)

        @pl.loop(0, 8, unroll=True)
        def _(n):
            lats = pl.ds(pl.multiple_of(512 * n, 512), 512)
            scores = lax.dot_general(dec2[lats, :], errors, NT, preferred_element_type=F32)
            for i, g in enumerate(groups):
                where = key_t[:, pl.ds(pl.multiple_of(512 * core + 128 * g, 128), 128)]
                total = grad_part[g]
                for b in range(8):
                    total += jnp.where(
                        where == 8 * n + b, scores[64 * b:64 * b + 64, 128 * i:128 * i + 128], 0.0)
                grad_part[g] = total

    recon(0)
    recon(1)
    for o in ORDER:
        forwards[o].wait_recv()

    @pl.loop(0, 8)
    def _(j):
        block = pl.ds(pl.multiple_of(128 * j, 128), 128)
        cols_t[block, :] = cols[:, block].T

    store_cols = pltpu.make_async_copy(cols_t, cols_out, sem_local.at[6])
    store_cols.start()
    error(0)
    error(1)
    code_grad(0)
    code_grad(1)

    grads = {}
    for o in ORDER:
        to = along(o)
        grads[o] = remote(grad_part.at[to], grad_recv.at[o], sem_d, o, (to, lat))
        grads[o].start()

    swap_codes.wait_recv()
    for chunk in range(2):
        across[chunk].wait_recv()

    def tile(n):
        return pl.ds(pl.multiple_of(256 * n, 256), 256)

    def dec_grads(first, last):
        values = jnp.concatenate(
            [codes[h, g].astype(F32) for h in range(2) for g in range(4)], axis=1)
        errors = err[...].reshape(1024, 1024)

        @pl.loop(first, last, unroll=True)
        def _(n):
            where = key_t[...]
            wide = jnp.concatenate(
                [jnp.where(where == 32 * core + 4 * n + b, values, 0.0).astype(BF16) for b in range(4)], axis=0)
            dec_grad_v[tile(n), :] = jnp.dot(wide, errors, preferred_element_type=F32).astype(BF16)
            pltpu.make_async_copy(dec_grad_v.at[tile(n)], dec_grad_out.at[tile(n)], sem_o.at[n]).start()

    dec_grads(0, 4)
    total = grad_part[z]
    for o in ORDER:
        grads[o].wait_recv()
        total = total + grad_recv[o]
    grad_out[core, z] = total
    shares = []
    for o in (0,) + ORDER:
        if o:
            shares.append(remote(grad_out.at[core, z], grad_out.at[core, z], sem_e, o, (along(o), lat)))
            shares[-1].start()
        shares.append(remote(grad_out.at[core, z], grad_out.at[core, z], sem_e, 4 + o, (along(o), sib_lat)))
        shares[-1].start()
    dec_grads(4, 8)
    bias_out[...] = jnp.dot(
        jnp.ones((16, 1024), BF16), err[...].reshape(1024, 1024), preferred_element_type=F32)[:1]

    for copy in shares:
        copy.wait()
    for o in ORDER:
        for group in (forwards, returns, shared, grads):
            group[o].wait_send()
    for copy in [sends[2], give_bias, give_dec, swap_codes] + list(scatter.values()) + list(gather.values()) + list(across.values()):
        copy.wait_send()
    store_cols.wait()

    @pl.loop(0, 8)
    def _(n):
        pltpu.make_async_copy(dec_grad_v.at[tile(n)], dec_grad_out.at[tile(n)], sem_o.at[n]).wait()


def enc_grads(cols_t, grad, idx_t, lat_ref, dec_in, enc_out, enc_bias_out, dec_out, wide, sem):
    n = pl.program_id(0)

    @pl.when(n == 0)
    def _():
        pltpu.make_async_copy(dec_in, dec_out, sem).start()
        odd = (lax.broadcasted_iota(I32, (128, 128), 1) >= 64).astype(I32)
        sums = [jnp.zeros((1, 128), F32)] * 16
        for g in range(8):
            piece = lax.shift_right_logical(idx_t[:, 128 * g:128 * g + 128], 6) - 32 * lat_ref[0]
            where = jnp.concatenate([piece, piece], axis=0).T - odd
            piece = grad[g % 2, g // 2]
            values = jnp.concatenate([piece, piece], axis=0).T
            for j in range(16):
                part = jnp.where(where == 2 * j, values, 0.0)
                sums[j] = sums[j] + jnp.sum(part, axis=0, keepdims=True)
                wide[128 * g:128 * g + 128, 128 * j:128 * j + 128] = part.astype(BF16)
        for j in range(16):
            enc_bias_out[:, 128 * j:128 * j + 128] = sums[j]

    tile = pl.ds(pl.multiple_of(512 * n, 512), 512)
    enc_out[...] = jnp.dot(cols_t[...], wide[:, tile], preferred_element_type=F32).astype(BF16)

    @pl.when(n == 3)
    def _():
        pltpu.make_async_copy(dec_in, dec_out, sem).wait()


def local(tokens, indices, enc_weight, dec_weight, enc_bias, dec_bias):
    idx_t = indices.T
    vmem = pl.BlockSpec(memory_space=pltpu.VMEM)
    hbm = pl.BlockSpec(memory_space=pltpu.HBM)
    free = pl.BlockSpec(memory_space=pl.ANY)
    dma = pltpu.SemaphoreType.DMA
    cols_t, dec_grad, grad, bias_grad = pl.pallas_call(
        exchange,
        out_shape=[
            jax.ShapeDtypeStruct((1024, 1024), BF16),
            jax.ShapeDtypeStruct((2048, 1024), BF16),
            jax.ShapeDtypeStruct((2, 4, 64, 128), F32),
            jax.ShapeDtypeStruct((1, 1024), F32),
        ],
        in_specs=[hbm] * 6,
        out_specs=[free, free, vmem, vmem],
        scratch_shapes=[
            pltpu.VMEM((64, 1024), I32),
            pltpu.VMEM((2, 1, 2048), F32),
            pltpu.VMEM((1, 1024), F32),
            pltpu.VMEM((1024, 1024), BF16),
            pltpu.VMEM((2048, 2048), BF16),
            pltpu.VMEM((4096, 1024), BF16),
            pltpu.VMEM((4, 128, 128), I32),
            pltpu.VMEM((64, 1024), I32),
            pltpu.VMEM((4, 128, 128), F32),
            pltpu.VMEM((64, 128), F32),
            pltpu.VMEM((4, 64, 128), F32),
            pltpu.VMEM((4, 64, 128), F32),
            pltpu.VMEM((2, 4, 64, 128), BF16),
            pltpu.VMEM((256, 4096), BF16),
            pltpu.VMEM((1024, 1024), BF16),
            pltpu.VMEM((512, 1024), BF16),
            pltpu.VMEM((32, 16, 1024), BF16),
            pltpu.VMEM((2, 512, 1024), BF16),
            pltpu.VMEM((4, 64, 128), F32),
            pltpu.VMEM((4, 64, 128), F32),
            pltpu.VMEM((2048, 1024), BF16),
            dma((7,)), dma((2, 4)), dma((2, 3)), dma((2, 4)), dma((2, 4)), dma((2, 4)), dma((2, 1)),
            dma((2, 32)), dma((2, 32)), dma((2, 2)), dma((2, 4)), dma((2, 8)), dma((8,)),
        ],
        compiler_params=pltpu.CompilerParams(
            collective_id=0, has_side_effects=True, vmem_limit_bytes=42 * 2**20),
        name="exchange",
    )(*[pltpu.with_memory_space_constraint(a, pltpu.HBM) for a in (
        tokens, idx_t, enc_weight, dec_weight, enc_bias[None, :], dec_bias[None, :])])

    enc_grad, enc_bias_grad, dec_grad = pl.pallas_call(
        enc_grads,
        grid=(4,),
        out_shape=[
            jax.ShapeDtypeStruct((1024, 2048), BF16),
            jax.ShapeDtypeStruct((1, 2048), F32),
            jax.ShapeDtypeStruct((2048, 1024), BF16),
        ],
        in_specs=[
            vmem,
            vmem,
            vmem,
            pl.BlockSpec(memory_space=pltpu.SMEM),
            free,
        ],
        out_specs=[
            pl.BlockSpec((1024, 512), lambda n: (0, n)),
            pl.BlockSpec((1, 2048), lambda n: (0, 0)),
            hbm,
        ],
        scratch_shapes=[pltpu.VMEM((1024, 2048), BF16), dma(())],
        compiler_params=pltpu.CompilerParams(vmem_limit_bytes=40 * 2**20),
        name="enc_grads",
    )(cols_t, grad, idx_t, lax.axis_index("lat").reshape(1), dec_grad)
    return enc_grad, dec_grad, enc_bias_grad[0], bias_grad[0]


def solution(mesh):
    placed = (P("tok", None), P(), P("tok", "lat"), P("lat", "tok"), P("lat"), P("tok"))
    return jax.shard_map(
        local,
        mesh=mesh,
        in_specs=placed,
        out_specs=(P("tok", "lat"), P("lat", "tok"), P("lat"), P("tok")),
        check_vma=False,
    )
```

```python
import jax
import jax.numpy as jnp
from jax import lax
from jax.experimental import pallas as pl
from jax.experimental.pallas import tpu as pltpu
from jax.sharding import PartitionSpec as P

MESH = pl.DeviceIdType.MESH
F32, BF16, I32 = jnp.float32, jnp.bfloat16, jnp.int32
NT = (((1,), (1,)), ((), ()))
PLANE = tuple((dy, dx) for dy in range(4) for dx in range(4))
ORDER = (1, 3, 2)


def exchange(
    tokens, idx_in, enc, dec, enc_bias, dec_bias,
    cols_out, dec_grad_out, grad_out, bias_out,
    idx_t, bias_e, bias_d, cols, enc2, dec2, key, key_t, picked, own_pre, pre_send, pre_recv,
    codes, dense, cols_t, rs_send, rs_recv, err, grad_part, grad_recv, dec_grad_v,
    sem_local, sem_a, sem_w, sem_f, sem_b, sem_c, sem_k, sem_r, sem_g, sem_h, sem_d, sem_e, sem_o,
):
    z, lat = lax.axis_index("tok"), lax.axis_index("lat")
    y, x, core = lat // 8, (lat // 2) % 4, lat % 2
    other = 1 - core
    sib_lat = lat + 1 - 2 * core
    sibling = (z, sib_lat)

    def along(offset):
        return lax.rem(z + offset, 4)

    def in_plane(dy, dx):
        return (z, lax.rem(y + dy, 4) * 8 + lax.rem(x + dx, 4) * 2 + core)

    def remote(src, dst, sems, index, device):
        return pltpu.make_async_remote_copy(
            src_ref=src, dst_ref=dst, send_sem=sems.at[0, index], recv_sem=sems.at[1, index],
            device_id=device, device_id_type=MESH,
        )

    barrier = pltpu.get_barrier_semaphore()
    peers = [(along(o), lat) for o in ORDER] + [sibling]
    peers += [(along(o), sib_lat) for o in ORDER]
    peers += [in_plane(dy, dx) for dy, dx in PLANE if dy or dx]
    for peer in peers:
        pl.semaphore_signal(barrier, inc=1, device_id=peer, device_id_type=MESH)

    enc_rows = pl.ds(pl.multiple_of(1024 * core, 1024), 1024)
    dec_rows = pl.ds(pl.multiple_of(2048 * core, 2048), 2048)
    loads = [
        pltpu.make_async_copy(
            tokens.at[:, pl.ds(pl.multiple_of(1024 * z, 1024), 1024)],
            cols.at[pl.ds(pl.multiple_of(256 * z, 256), 256)], sem_local.at[0]),
        pltpu.make_async_copy(idx_in, idx_t, sem_local.at[1]),
        pltpu.make_async_copy(enc_bias, bias_e.at[core], sem_local.at[2]),
        pltpu.make_async_copy(enc, enc2.at[enc_rows], sem_local.at[3]),
        pltpu.make_async_copy(dec_bias, bias_d, sem_local.at[4]),
        pltpu.make_async_copy(dec, dec2.at[dec_rows], sem_local.at[5]),
    ]
    for copy in loads:
        copy.start()

    pl.semaphore_wait(barrier, len(peers))

    def half(block, which):
        return pl.ds(pl.multiple_of(256 * block + 128 * which, 128), 128)

    sends = {}
    for o in ORDER:
        to = along(o)
        sends[o] = remote(
            tokens.at[pl.ds(pl.multiple_of(128 * core, 128), 128), pl.ds(pl.multiple_of(1024 * to, 1024), 1024)],
            cols.at[half(z, core)], sem_a, o, (to, lat))
        if o != 2:
            sends[o].start()
    give_bias = remote(enc_bias, bias_e.at[core], sem_w, 0, sibling)
    give_enc = remote(enc, enc2.at[enc_rows], sem_w, 1, sibling)
    give_dec = remote(dec, dec2.at[dec_rows], sem_w, 2, sibling)
    give_bias.start()
    give_enc.start()

    loads[1].wait()
    odd = (lax.broadcasted_iota(I32, (128, 128), 1) >= 64).astype(I32)
    for g in range(4):
        for h in range(2):
            at = 256 * g + 128 * h
            band = lax.shift_right_logical(idx_t[:, at:at + 128], 6) - 64 * (lat // 2)
            key_t[:, 512 * h + 128 * g:512 * h + 128 * g + 128] = band
        band = lax.shift_right_logical(idx_t[:, half(g, core)], 6) - 64 * (lat // 2)
        key[g] = jnp.concatenate([band, band], axis=0).T - odd

    def pick(blocks, which, bias_first):
        rows = jnp.concatenate([cols[half(b, core), :] for b in blocks], axis=0) if len(blocks) > 1 else cols[half(blocks[0], core), :]
        weights = pl.ds(pl.multiple_of(1024 * which, 1024), 1024)

        @pl.loop(0, 4, unroll=True)
        def _(n):
            base = pl.multiple_of(512 * n, 512)
            scores = jnp.dot(rows, enc2[weights, pl.ds(base, 512)], preferred_element_type=F32)
            if bias_first:
                scores = scores + bias_e[which, :, pl.ds(base, 512)]
            for i, b in enumerate(blocks):
                where = key[b]
                total = picked[b]
                for j in range(4):
                    total += jnp.where(
                        where == 32 * which + 8 * n + 2 * j,
                        scores[128 * i:128 * i + 128, 128 * j:128 * j + 128], 0.0)
                picked[b] = total

    def folded(block):
        turned = picked[block].T
        return turned[:64] + turned[64:]

    picked[...] = jnp.zeros_like(picked)
    loads[0].wait()
    loads[2].wait()
    loads[3].wait()
    pick([z], core, True)

    returns = {}
    forwards = {}

    def forward(o):
        rows = half(along(4 - o), core)
        forwards[o] = remote(cols.at[rows], cols.at[rows], sem_f, o, sibling)
        forwards[o].start()

    def give_back(o):
        pre_send[o] = folded(along(4 - o))
        returns[o] = remote(pre_send.at[o], pre_recv.at[o], sem_b, o, (along(4 - o), lat))
        returns[o].start()

    sends[1].wait_send()
    sends[3].wait_send()
    sends[2].start()
    sends[1].wait_recv()
    sends[3].wait_recv()
    pair = [along(3), along(1)]
    pick(pair, core, False)
    give_bias.wait_recv()
    give_enc.wait()
    give_dec.start()
    pick(pair, other, False)
    give_back(1)
    give_back(3)
    pick([z], other, True)
    own_pre[...] = folded(z)
    sends[2].wait_recv()
    last = [along(2)]
    pick(last, core, False)
    pick(last, other, False)
    give_back(2)
    for o in ORDER:
        forward(o)

    total = own_pre[...]
    for o in ORDER:
        returns[o].wait_recv()
        total = total + pre_recv[o]
    codes[core, z] = total.astype(BF16)
    shared = {}
    for o in ORDER:
        shared[o] = remote(codes.at[core, z], codes.at[core, z], sem_c, o, (along(o), lat))
        shared[o].start()
    for copy in loads[4:]:
        copy.wait()
    give_dec.wait_recv()
    for o in ORDER:
        shared[o].wait_recv()
    swap_codes = remote(codes.at[core], codes.at[core], sem_k, 0, sibling)
    swap_codes.start()

    spot = 4 * y + x
    scatter, gather, across = {}, {}, {}

    def share(chunk, place):
        return pl.ds(pl.multiple_of(256 * chunk + 16 * place, 16), 16)

    def partners(chunk):
        for slot in range(1, 16):
            dy, dx = PLANE[slot]
            place = 4 * lax.rem(y + dy, 4) + lax.rem(x + dx, 4)
            yield 16 * chunk + slot, place, in_plane(dy, dx)

    def recon(chunk):
        for pos in range(2):
            turned = codes[core, 2 * chunk + pos].astype(F32)
            values = jnp.concatenate([turned, turned], axis=0).T
            where = key[2 * chunk + pos]
            for j in range(32):
                dense[128 * pos:128 * pos + 128, 128 * j:128 * j + 128] = jnp.where(
                    where == 2 * j, values, 0.0).astype(BF16)

        rows = slice(256 * chunk, 256 * chunk + 256)
        for n in range(2):
            base = slice(512 * n, 512 * n + 512)
            rs_send[rows, base] = jnp.dot(
                dense[...], dec2[:, base], preferred_element_type=F32).astype(BF16)
            if chunk == 1 and n == 0:
                continue
            base = base if chunk == 0 else slice(0, 1024)
            for slot, place, device in partners(chunk):
                scatter[slot, n] = remote(
                    rs_send.at[share(chunk, place), base], rs_recv.at[slot, :, base], sem_r,
                    slot + 32 * (n if chunk == 0 else 0), device)
                scatter[slot, n].start()

    def error(chunk):
        mine = share(chunk, spot)
        rows = pl.ds(pl.multiple_of(512 * chunk + 256 * (spot // 8) + 128 * core + 16 * lax.rem(spot, 8), 16), 16)
        full = rs_send[mine, :].astype(F32) + bias_d[...]
        full = full - cols[rows, :].astype(F32)
        for slot in range(16 * chunk + 1, 16 * chunk + 16):
            for n in range(chunk, 2):
                scatter[slot, n].wait_recv()
            full = full + rs_recv[slot].astype(F32)
        err[core, mine, :] = full.astype(BF16)
        for slot, _, device in partners(chunk):
            gather[slot] = remote(err.at[core, mine], err.at[core, mine], sem_g, slot, device)
            gather[slot].start()

    def code_grad(chunk):
        for slot in range(16 * chunk + 1, 16 * chunk + 16):
            gather[slot].wait_recv()
        rows = slice(256 * chunk, 256 * chunk + 256)
        across[chunk] = remote(err.at[core, rows], err.at[core, rows], sem_h, chunk, sibling)
        across[chunk].start()
        errors = err[core, rows, :]
        groups = (2 * chunk, 2 * chunk + 1)
        for g in groups:
            grad_part[g] = jnp.zeros((64, 128), F32)

        @pl.loop(0, 8, unroll=True)
        def _(n):
            lats = pl.ds(pl.multiple_of(512 * n, 512), 512)
            scores = lax.dot_general(dec2[lats, :], errors, NT, preferred_element_type=F32)
            for i, g in enumerate(groups):
                where = key_t[:, pl.ds(pl.multiple_of(512 * core + 128 * g, 128), 128)]
                total = grad_part[g]
                for b in range(8):
                    total += jnp.where(
                        where == 8 * n + b, scores[64 * b:64 * b + 64, 128 * i:128 * i + 128], 0.0)
                grad_part[g] = total

    recon(0)
    recon(1)
    for o in ORDER:
        forwards[o].wait_recv()

    @pl.loop(0, 8)
    def _(j):
        block = pl.ds(pl.multiple_of(128 * j, 128), 128)
        cols_t[block, :] = cols[:, block].T

    store_cols = pltpu.make_async_copy(cols_t, cols_out, sem_local.at[6])
    store_cols.start()
    error(0)
    error(1)
    code_grad(0)
    code_grad(1)

    grads = {}
    for o in ORDER:
        to = along(o)
        grads[o] = remote(grad_part.at[to], grad_recv.at[o], sem_d, o, (to, lat))
        grads[o].start()

    swap_codes.wait_recv()
    for chunk in range(2):
        across[chunk].wait_recv()

    def tile(n):
        return pl.ds(pl.multiple_of(256 * n, 256), 256)

    def dec_grads(first, last):
        values = jnp.concatenate(
            [codes[h, g].astype(F32) for h in range(2) for g in range(4)], axis=1)
        errors = err[...].reshape(1024, 1024)

        @pl.loop(first, last, unroll=True)
        def _(n):
            where = key_t[...]
            wide = jnp.concatenate(
                [jnp.where(where == 32 * core + 4 * n + b, values, 0.0).astype(BF16) for b in range(4)], axis=0)
            dec_grad_v[tile(n), :] = jnp.dot(wide, errors, preferred_element_type=F32).astype(BF16)
            pltpu.make_async_copy(dec_grad_v.at[tile(n)], dec_grad_out.at[tile(n)], sem_o.at[n]).start()

    dec_grads(0, 4)
    total = grad_part[z]
    for o in ORDER:
        grads[o].wait_recv()
        total = total + grad_recv[o]
    grad_out[core, z] = total
    shares = []
    for o in (0,) + ORDER:
        if o:
            shares.append(remote(grad_out.at[core, z], grad_out.at[core, z], sem_e, o, (along(o), lat)))
            shares[-1].start()
        shares.append(remote(grad_out.at[core, z], grad_out.at[core, z], sem_e, 4 + o, (along(o), sib_lat)))
        shares[-1].start()
    dec_grads(4, 8)
    bias_out[...] = jnp.dot(
        jnp.ones((16, 1024), BF16), err[...].reshape(1024, 1024), preferred_element_type=F32)[:1]

    for copy in shares:
        copy.wait()
    for o in ORDER:
        for group in (forwards, returns, shared, grads):
            group[o].wait_send()
    for copy in [sends[2], give_bias, give_dec, swap_codes] + list(scatter.values()) + list(gather.values()) + list(across.values()):
        copy.wait_send()
    store_cols.wait()

    @pl.loop(0, 8)
    def _(n):
        pltpu.make_async_copy(dec_grad_v.at[tile(n)], dec_grad_out.at[tile(n)], sem_o.at[n]).wait()


def enc_grads(
    cols_t, grad, idx_t, bias_in, lat_ref, dec_in, enc_out, enc_bias_out, bias_out, dec_out, key, values, wide, enc_v, sem
):
    pass_dec = pltpu.make_async_copy(dec_in, dec_out, sem.at[4])
    pass_dec.start()
    bias_out[...] = bias_in[...]
    odd = (lax.broadcasted_iota(I32, (128, 128), 1) >= 64).astype(I32)
    for g in range(8):
        piece = lax.shift_right_logical(idx_t[:, 128 * g:128 * g + 128], 6) - 32 * lat_ref[0]
        key[128 * g:128 * g + 128, :] = jnp.concatenate([piece, piece], axis=0).T - odd
        piece = grad[g % 2, g // 2]
        values[128 * g:128 * g + 128, :] = jnp.concatenate([piece, piece], axis=0).T

    stores = []
    for n in range(4):
        for j in range(4 * n, 4 * n + 4):
            part = jnp.where(key[...] == 2 * j, values[...], 0.0)
            enc_bias_out[:, 128 * j:128 * j + 128] = jnp.sum(part, axis=0, keepdims=True)
            wide[:, 128 * j:128 * j + 128] = part.astype(BF16)
        tile = slice(512 * n, 512 * n + 512)
        enc_v[n] = jnp.dot(cols_t[...], wide[:, tile], preferred_element_type=F32).astype(BF16)
        stores.append(pltpu.make_async_copy(enc_v.at[n], enc_out.at[:, tile], sem.at[n]))
        stores[n].start()
    for copy in stores + [pass_dec]:
        copy.wait()


def local(tokens, indices, enc_weight, dec_weight, enc_bias, dec_bias):
    idx_t = indices.T
    vmem = pl.BlockSpec(memory_space=pltpu.VMEM)
    hbm = pl.BlockSpec(memory_space=pltpu.HBM)
    free = pl.BlockSpec(memory_space=pl.ANY)
    dma = pltpu.SemaphoreType.DMA
    cols_t, dec_grad, grad, bias_grad = pl.pallas_call(
        exchange,
        out_shape=[
            jax.ShapeDtypeStruct((1024, 1024), BF16),
            jax.ShapeDtypeStruct((2048, 1024), BF16),
            jax.ShapeDtypeStruct((2, 4, 64, 128), F32),
            jax.ShapeDtypeStruct((1, 1024), F32),
        ],
        in_specs=[hbm] * 6,
        out_specs=[free, free, vmem, vmem],
        scratch_shapes=[
            pltpu.VMEM((64, 1024), I32),
            pltpu.VMEM((2, 1, 2048), F32),
            pltpu.VMEM((1, 1024), F32),
            pltpu.VMEM((1024, 1024), BF16),
            pltpu.VMEM((2048, 2048), BF16),
            pltpu.VMEM((4096, 1024), BF16),
            pltpu.VMEM((4, 128, 128), I32),
            pltpu.VMEM((64, 1024), I32),
            pltpu.VMEM((4, 128, 128), F32),
            pltpu.VMEM((64, 128), F32),
            pltpu.VMEM((4, 64, 128), F32),
            pltpu.VMEM((4, 64, 128), F32),
            pltpu.VMEM((2, 4, 64, 128), BF16),
            pltpu.VMEM((256, 4096), BF16),
            pltpu.VMEM((1024, 1024), BF16),
            pltpu.VMEM((512, 1024), BF16),
            pltpu.VMEM((32, 16, 1024), BF16),
            pltpu.VMEM((2, 512, 1024), BF16),
            pltpu.VMEM((4, 64, 128), F32),
            pltpu.VMEM((4, 64, 128), F32),
            pltpu.VMEM((2048, 1024), BF16),
            dma((7,)), dma((2, 4)), dma((2, 3)), dma((2, 4)), dma((2, 4)), dma((2, 4)), dma((2, 1)),
            dma((2, 48)), dma((2, 32)), dma((2, 2)), dma((2, 4)), dma((2, 8)), dma((8,)),
        ],
        compiler_params=pltpu.CompilerParams(
            collective_id=0, has_side_effects=True, vmem_limit_bytes=42 * 2**20),
        name="exchange",
    )(*[pltpu.with_memory_space_constraint(a, pltpu.HBM) for a in (
        tokens, idx_t, enc_weight, dec_weight, enc_bias[None, :], dec_bias[None, :])])

    enc_grad, enc_bias_grad, bias_grad, dec_grad = pl.pallas_call(
        enc_grads,
        out_shape=[
            jax.ShapeDtypeStruct((1024, 2048), BF16),
            jax.ShapeDtypeStruct((1, 2048), F32),
            jax.ShapeDtypeStruct((1, 1024), F32),
            jax.ShapeDtypeStruct((2048, 1024), BF16),
        ],
        in_specs=[vmem, vmem, vmem, vmem, pl.BlockSpec(memory_space=pltpu.SMEM), free],
        out_specs=[hbm, vmem, vmem, hbm],
        scratch_shapes=[
            pltpu.VMEM((1024, 128), I32),
            pltpu.VMEM((1024, 128), F32),
            pltpu.VMEM((1024, 2048), BF16),
            pltpu.VMEM((4, 1024, 512), BF16),
            dma((5,)),
        ],
        compiler_params=pltpu.CompilerParams(vmem_limit_bytes=40 * 2**20),
        name="enc_grads",
    )(cols_t, grad, idx_t, bias_grad, lax.axis_index("lat").reshape(1), dec_grad)
    return enc_grad, dec_grad, enc_bias_grad[0], bias_grad[0]


def solution(mesh):
    placed = (P("tok", None), P(), P("tok", "lat"), P("lat", "tok"), P("lat"), P("tok"))
    return jax.shard_map(
        local,
        mesh=mesh,
        in_specs=placed,
        out_specs=(P("tok", "lat"), P("lat", "tok"), P("lat"), P("tok")),
        check_vma=False,
    )
```

```python
import jax
import jax.numpy as jnp
from jax import lax
from jax.experimental import pallas as pl
from jax.experimental.pallas import tpu as pltpu
from jax.sharding import PartitionSpec as P

MESH = pl.DeviceIdType.MESH
F32, BF16, I32 = jnp.float32, jnp.bfloat16, jnp.int32
NT = (((1,), (1,)), ((), ()))
PLANE = tuple((dy, dx) for dy in range(4) for dx in range(4))
ORDER = (1, 3, 2)


def exchange(
    tokens, idx_in, enc, dec, enc_bias, dec_bias,
    cols_out, dec_grad_out, grad_out, bias_out,
    idx_t, bias_e, bias_d, cols, enc2, dec2, key, key_t, picked, own_pre, pre_send, pre_recv,
    codes, dense, cols_t, rs_send, rs_recv, err, grad_part, grad_recv, dec_grad_v,
    sem_local, sem_a, sem_w, sem_f, sem_b, sem_c, sem_k, sem_r, sem_g, sem_h, sem_d, sem_e, sem_o,
):
    z, lat = lax.axis_index("tok"), lax.axis_index("lat")
    y, x, core = lat // 8, (lat // 2) % 4, lat % 2
    other = 1 - core
    sib_lat = lat + 1 - 2 * core
    sibling = (z, sib_lat)

    def along(offset):
        return lax.rem(z + offset, 4)

    def in_plane(dy, dx):
        return (z, lax.rem(y + dy, 4) * 8 + lax.rem(x + dx, 4) * 2 + core)

    def remote(src, dst, sems, index, device):
        return pltpu.make_async_remote_copy(
            src_ref=src, dst_ref=dst, send_sem=sems.at[0, index], recv_sem=sems.at[1, index],
            device_id=device, device_id_type=MESH,
        )

    barrier = pltpu.get_barrier_semaphore()
    peers = [(along(o), lat) for o in ORDER] + [sibling]
    peers += [(along(o), sib_lat) for o in ORDER]
    peers += [in_plane(dy, dx) for dy, dx in PLANE if dy or dx]
    for peer in peers:
        pl.semaphore_signal(barrier, inc=1, device_id=peer, device_id_type=MESH)

    enc_rows = pl.ds(pl.multiple_of(1024 * core, 1024), 1024)
    dec_rows = pl.ds(pl.multiple_of(2048 * core, 2048), 2048)
    loads = [
        pltpu.make_async_copy(
            tokens.at[:, pl.ds(pl.multiple_of(1024 * z, 1024), 1024)],
            cols.at[pl.ds(pl.multiple_of(256 * z, 256), 256)], sem_local.at[0]),
        pltpu.make_async_copy(idx_in, idx_t, sem_local.at[1]),
        pltpu.make_async_copy(enc_bias, bias_e.at[core], sem_local.at[2]),
        pltpu.make_async_copy(enc, enc2.at[enc_rows], sem_local.at[3]),
        pltpu.make_async_copy(dec_bias, bias_d, sem_local.at[4]),
        pltpu.make_async_copy(dec, dec2.at[dec_rows], sem_local.at[5]),
    ]
    for copy in loads:
        copy.start()

    pl.semaphore_wait(barrier, len(peers))

    def half(block, which):
        return pl.ds(pl.multiple_of(256 * block + 128 * which, 128), 128)

    sends = {}
    for o in ORDER:
        to = along(o)
        sends[o] = remote(
            tokens.at[pl.ds(pl.multiple_of(128 * core, 128), 128), pl.ds(pl.multiple_of(1024 * to, 1024), 1024)],
            cols.at[half(z, core)], sem_a, o, (to, lat))
        if o != 2:
            sends[o].start()
    give_bias = remote(enc_bias, bias_e.at[core], sem_w, 0, sibling)
    give_enc = remote(enc, enc2.at[enc_rows], sem_w, 1, sibling)
    give_dec = remote(dec, dec2.at[dec_rows], sem_w, 2, sibling)
    give_bias.start()
    give_enc.start()

    loads[1].wait()
    odd = (lax.broadcasted_iota(I32, (128, 128), 1) >= 64).astype(I32)
    for g in range(4):
        for h in range(2):
            at = 256 * g + 128 * h
            band = lax.shift_right_logical(idx_t[:, at:at + 128], 6) - 64 * (lat // 2)
            key_t[:, 512 * h + 128 * g:512 * h + 128 * g + 128] = band
        band = lax.shift_right_logical(idx_t[:, half(g, core)], 6) - 64 * (lat // 2)
        key[g] = jnp.concatenate([band, band], axis=0).T - odd

    def pick(blocks, which, bias_first):
        rows = jnp.concatenate([cols[half(b, core), :] for b in blocks], axis=0) if len(blocks) > 1 else cols[half(blocks[0], core), :]
        weights = pl.ds(pl.multiple_of(1024 * which, 1024), 1024)

        @pl.loop(0, 4, unroll=True)
        def _(n):
            base = pl.multiple_of(512 * n, 512)
            scores = jnp.dot(rows, enc2[weights, pl.ds(base, 512)], preferred_element_type=F32)
            if bias_first:
                scores = scores + bias_e[which, :, pl.ds(base, 512)]
            for i, b in enumerate(blocks):
                where = key[b]
                total = picked[b]
                for j in range(4):
                    total += jnp.where(
                        where == 32 * which + 8 * n + 2 * j,
                        scores[128 * i:128 * i + 128, 128 * j:128 * j + 128], 0.0)
                picked[b] = total

    def folded(block):
        turned = picked[block].T
        return turned[:64] + turned[64:]

    picked[...] = jnp.zeros_like(picked)
    loads[0].wait()
    loads[2].wait()
    loads[3].wait()
    pick([z], core, True)

    returns = {}
    forwards = {}

    def forward(o):
        rows = half(along(4 - o), core)
        forwards[o] = remote(cols.at[rows], cols.at[rows], sem_f, o, sibling)
        forwards[o].start()

    def give_back(o):
        pre_send[o] = folded(along(4 - o))
        returns[o] = remote(pre_send.at[o], pre_recv.at[o], sem_b, o, (along(4 - o), lat))
        returns[o].start()

    sends[1].wait_send()
    sends[3].wait_send()
    sends[2].start()
    sends[1].wait_recv()
    sends[3].wait_recv()
    pair = [along(3), along(1)]
    pick(pair, core, False)
    give_bias.wait_recv()
    give_enc.wait()
    give_dec.start()
    pick(pair, other, False)
    give_back(1)
    give_back(3)
    pick([z], other, True)
    own_pre[...] = folded(z)
    sends[2].wait_recv()
    last = [along(2)]
    pick(last, core, False)
    pick(last, other, False)
    give_back(2)
    for o in ORDER:
        forward(o)

    total = own_pre[...]
    for o in ORDER:
        returns[o].wait_recv()
        total = total + pre_recv[o]
    codes[core, z] = total.astype(BF16)
    shared = {}
    for o in ORDER:
        shared[o] = remote(codes.at[core, z], codes.at[core, z], sem_c, o, (along(o), lat))
        shared[o].start()
    for copy in loads[4:]:
        copy.wait()
    give_dec.wait_recv()
    for o in ORDER:
        shared[o].wait_recv()
    swap_codes = remote(codes.at[core], codes.at[core], sem_k, 0, sibling)
    swap_codes.start()

    near, far = jnp.where(core == 0, x, y), jnp.where(core == 0, y, x)
    spot = 4 * near + far
    scatter, gather, across = {}, {}, {}

    def first(o):
        return in_plane(o * core, o * other)

    def second(o):
        return in_plane(o * other, o * core)

    def share(chunk, place):
        return pl.ds(pl.multiple_of(256 * chunk + 16 * place, 16), 16)

    def partners(chunk):
        for slot in range(1, 16):
            dy, dx = PLANE[slot]
            row, column = lax.rem(y + dy, 4), lax.rem(x + dx, 4)
            place = jnp.where(core == 0, 4 * column + row, 4 * row + column)
            yield 16 * chunk + slot, place, in_plane(dy, dx)

    def recon(chunk):
        for pos in range(2):
            turned = codes[core, 2 * chunk + pos].astype(F32)
            values = jnp.concatenate([turned, turned], axis=0).T
            where = key[2 * chunk + pos]
            for j in range(32):
                dense[128 * pos:128 * pos + 128, 128 * j:128 * j + 128] = jnp.where(
                    where == 2 * j, values, 0.0).astype(BF16)

        rows = slice(256 * chunk, 256 * chunk + 256)
        for n in range(2):
            base = slice(512 * n, 512 * n + 512)
            rs_send[rows, base] = jnp.dot(
                dense[...], dec2[:, base], preferred_element_type=F32).astype(BF16)
            if chunk == 1 and n == 0:
                continue
            base = base if chunk == 0 else slice(0, 1024)
            for slot, place, device in partners(chunk):
                scatter[slot, n] = remote(
                    rs_send.at[share(chunk, place), base], rs_recv.at[slot, :, base], sem_r,
                    slot + 32 * (n if chunk == 0 else 0), device)
                scatter[slot, n].start()

    def error(chunk):
        mine = share(chunk, spot)
        rows = pl.ds(pl.multiple_of(512 * chunk + 256 * (spot // 8) + 128 * core + 16 * lax.rem(spot, 8), 16), 16)
        full = rs_send[mine, :].astype(F32) + bias_d[...]
        full = full - cols[rows, :].astype(F32)
        for slot in range(16 * chunk + 1, 16 * chunk + 16):
            for n in range(chunk, 2):
                scatter[slot, n].wait_recv()
            full = full + rs_recv[slot].astype(F32)
        err[core, mine, :] = full.astype(BF16)
        for o in ORDER:
            gather[chunk, 0, o] = remote(
                err.at[core, mine], err.at[core, mine], sem_g, 16 * chunk + o, second(o))
            gather[chunk, 0, o].start()
        hand_on(chunk, mine, 0)

    def hand_on(chunk, rows, source):
        for o in ORDER:
            gather[chunk, o, source] = remote(
                err.at[core, rows], err.at[core, rows], sem_g, 16 * chunk + 4 * o + source, first(o))
            gather[chunk, o, source].start()

    def pass_on(chunk):
        for source in ORDER:
            gather[chunk, 0, source].wait_recv()
            hand_on(chunk, share(chunk, 4 * near + lax.rem(far + 4 - source, 4)), source)

    def code_grad(chunk):
        for source in (0,) + ORDER:
            for o in ORDER:
                gather[chunk, o, source].wait_recv()
        rows = slice(256 * chunk, 256 * chunk + 256)
        across[chunk] = remote(err.at[core, rows], err.at[core, rows], sem_h, chunk, sibling)
        across[chunk].start()
        errors = err[core, rows, :]
        groups = (2 * chunk, 2 * chunk + 1)
        for g in groups:
            grad_part[g] = jnp.zeros((64, 128), F32)

        @pl.loop(0, 8, unroll=True)
        def _(n):
            lats = pl.ds(pl.multiple_of(512 * n, 512), 512)
            scores = lax.dot_general(dec2[lats, :], errors, NT, preferred_element_type=F32)
            for i, g in enumerate(groups):
                where = key_t[:, pl.ds(pl.multiple_of(512 * core + 128 * g, 128), 128)]
                total = grad_part[g]
                for b in range(8):
                    total += jnp.where(
                        where == 8 * n + b, scores[64 * b:64 * b + 64, 128 * i:128 * i + 128], 0.0)
                grad_part[g] = total

    recon(0)
    recon(1)
    for o in ORDER:
        forwards[o].wait_recv()

    @pl.loop(0, 8)
    def _(j):
        block = pl.ds(pl.multiple_of(128 * j, 128), 128)
        cols_t[block, :] = cols[:, block].T

    store_cols = pltpu.make_async_copy(cols_t, cols_out, sem_local.at[6])
    store_cols.start()
    error(0)
    error(1)
    pass_on(0)
    pass_on(1)
    code_grad(0)
    code_grad(1)

    grads = {}
    for o in ORDER:
        to = along(o)
        grads[o] = remote(grad_part.at[to], grad_recv.at[o], sem_d, o, (to, lat))
        grads[o].start()

    swap_codes.wait_recv()
    for chunk in range(2):
        across[chunk].wait_recv()

    def tile(n):
        return pl.ds(pl.multiple_of(256 * n, 256), 256)

    def dec_grads(first, last):
        values = jnp.concatenate(
            [codes[h, g].astype(F32) for h in range(2) for g in range(4)], axis=1)
        errors = err[...].reshape(1024, 1024)

        @pl.loop(first, last, unroll=True)
        def _(n):
            where = key_t[...]
            wide = jnp.concatenate(
                [jnp.where(where == 32 * core + 4 * n + b, values, 0.0).astype(BF16) for b in range(4)], axis=0)
            dec_grad_v[tile(n), :] = jnp.dot(wide, errors, preferred_element_type=F32).astype(BF16)
            pltpu.make_async_copy(dec_grad_v.at[tile(n)], dec_grad_out.at[tile(n)], sem_o.at[n]).start()

    dec_grads(0, 4)
    total = grad_part[z]
    for o in ORDER:
        grads[o].wait_recv()
        total = total + grad_recv[o]
    grad_out[core, z] = total
    shares = []
    for o in (0,) + ORDER:
        if o:
            shares.append(remote(grad_out.at[core, z], grad_out.at[core, z], sem_e, o, (along(o), lat)))
            shares[-1].start()
        shares.append(remote(grad_out.at[core, z], grad_out.at[core, z], sem_e, 4 + o, (along(o), sib_lat)))
        shares[-1].start()
    dec_grads(4, 8)
    bias_out[...] = jnp.dot(
        jnp.ones((16, 1024), BF16), err[...].reshape(1024, 1024), preferred_element_type=F32)[:1]

    for copy in shares:
        copy.wait()
    for o in ORDER:
        for group in (forwards, returns, shared, grads):
            group[o].wait_send()
    for copy in [sends[2], give_bias, give_dec, swap_codes] + list(scatter.values()) + list(gather.values()) + list(across.values()):
        copy.wait_send()
    store_cols.wait()

    @pl.loop(0, 8)
    def _(n):
        pltpu.make_async_copy(dec_grad_v.at[tile(n)], dec_grad_out.at[tile(n)], sem_o.at[n]).wait()


def enc_grads(
    cols_t, grad, idx_t, bias_in, lat_ref, dec_in, enc_out, enc_bias_out, bias_out, dec_out, key, values, wide, enc_v, sem
):
    pass_dec = pltpu.make_async_copy(dec_in, dec_out, sem.at[4])
    pass_dec.start()
    bias_out[...] = bias_in[...]
    odd = (lax.broadcasted_iota(I32, (128, 128), 1) >= 64).astype(I32)
    for g in range(8):
        piece = lax.shift_right_logical(idx_t[:, 128 * g:128 * g + 128], 6) - 32 * lat_ref[0]
        key[128 * g:128 * g + 128, :] = jnp.concatenate([piece, piece], axis=0).T - odd
        piece = grad[g % 2, g // 2]
        values[128 * g:128 * g + 128, :] = jnp.concatenate([piece, piece], axis=0).T

    stores = []
    for n in range(4):
        for j in range(4 * n, 4 * n + 4):
            part = jnp.where(key[...] == 2 * j, values[...], 0.0)
            enc_bias_out[:, 128 * j:128 * j + 128] = jnp.sum(part, axis=0, keepdims=True)
            wide[:, 128 * j:128 * j + 128] = part.astype(BF16)
        tile = slice(512 * n, 512 * n + 512)
        enc_v[n] = jnp.dot(cols_t[...], wide[:, tile], preferred_element_type=F32).astype(BF16)
        stores.append(pltpu.make_async_copy(enc_v.at[n], enc_out.at[:, tile], sem.at[n]))
        stores[n].start()
    for copy in stores + [pass_dec]:
        copy.wait()


def local(tokens, indices, enc_weight, dec_weight, enc_bias, dec_bias):
    idx_t = indices.T
    vmem = pl.BlockSpec(memory_space=pltpu.VMEM)
    hbm = pl.BlockSpec(memory_space=pltpu.HBM)
    free = pl.BlockSpec(memory_space=pl.ANY)
    dma = pltpu.SemaphoreType.DMA
    cols_t, dec_grad, grad, bias_grad = pl.pallas_call(
        exchange,
        out_shape=[
            jax.ShapeDtypeStruct((1024, 1024), BF16),
            jax.ShapeDtypeStruct((2048, 1024), BF16),
            jax.ShapeDtypeStruct((2, 4, 64, 128), F32),
            jax.ShapeDtypeStruct((1, 1024), F32),
        ],
        in_specs=[hbm] * 6,
        out_specs=[free, free, vmem, vmem],
        scratch_shapes=[
            pltpu.VMEM((64, 1024), I32),
            pltpu.VMEM((2, 1, 2048), F32),
            pltpu.VMEM((1, 1024), F32),
            pltpu.VMEM((1024, 1024), BF16),
            pltpu.VMEM((2048, 2048), BF16),
            pltpu.VMEM((4096, 1024), BF16),
            pltpu.VMEM((4, 128, 128), I32),
            pltpu.VMEM((64, 1024), I32),
            pltpu.VMEM((4, 128, 128), F32),
            pltpu.VMEM((64, 128), F32),
            pltpu.VMEM((4, 64, 128), F32),
            pltpu.VMEM((4, 64, 128), F32),
            pltpu.VMEM((2, 4, 64, 128), BF16),
            pltpu.VMEM((256, 4096), BF16),
            pltpu.VMEM((1024, 1024), BF16),
            pltpu.VMEM((512, 1024), BF16),
            pltpu.VMEM((32, 16, 1024), BF16),
            pltpu.VMEM((2, 512, 1024), BF16),
            pltpu.VMEM((4, 64, 128), F32),
            pltpu.VMEM((4, 64, 128), F32),
            pltpu.VMEM((2048, 1024), BF16),
            dma((7,)), dma((2, 4)), dma((2, 3)), dma((2, 4)), dma((2, 4)), dma((2, 4)), dma((2, 1)),
            dma((2, 48)), dma((2, 32)), dma((2, 2)), dma((2, 4)), dma((2, 8)), dma((8,)),
        ],
        compiler_params=pltpu.CompilerParams(
            collective_id=0, has_side_effects=True, vmem_limit_bytes=42 * 2**20),
        name="exchange",
    )(*[pltpu.with_memory_space_constraint(a, pltpu.HBM) for a in (
        tokens, idx_t, enc_weight, dec_weight, enc_bias[None, :], dec_bias[None, :])])

    enc_grad, enc_bias_grad, bias_grad, dec_grad = pl.pallas_call(
        enc_grads,
        out_shape=[
            jax.ShapeDtypeStruct((1024, 2048), BF16),
            jax.ShapeDtypeStruct((1, 2048), F32),
            jax.ShapeDtypeStruct((1, 1024), F32),
            jax.ShapeDtypeStruct((2048, 1024), BF16),
        ],
        in_specs=[vmem, vmem, vmem, vmem, pl.BlockSpec(memory_space=pltpu.SMEM), free],
        out_specs=[hbm, vmem, vmem, hbm],
        scratch_shapes=[
            pltpu.VMEM((1024, 128), I32),
            pltpu.VMEM((1024, 128), F32),
            pltpu.VMEM((1024, 2048), BF16),
            pltpu.VMEM((4, 1024, 512), BF16),
            dma((5,)),
        ],
        compiler_params=pltpu.CompilerParams(vmem_limit_bytes=40 * 2**20),
        name="enc_grads",
    )(cols_t, grad, idx_t, bias_grad, lax.axis_index("lat").reshape(1), dec_grad)
    return enc_grad, dec_grad, enc_bias_grad[0], bias_grad[0]


def solution(mesh):
    placed = (P("tok", None), P(), P("tok", "lat"), P("lat", "tok"), P("lat"), P("tok"))
    return jax.shard_map(
        local,
        mesh=mesh,
        in_specs=placed,
        out_specs=(P("tok", "lat"), P("lat", "tok"), P("lat"), P("tok")),
        check_vma=False,
    )
```
